32 devices in a mesh: seq: 8 (over z, x), tensor: 4 (over y, core).
Axes of the slice: x: 2, y: 2, z: 4, core: 2. Of those that a mesh axis runs over, the one named last changes fastest.
Arguments:
- queries: bfloat16 [512, 2048], P('seq', 'tensor'), may hold values from -5 to 5
- draft_keys: bfloat16 [512, 2048], P('seq', 'tensor'), may hold values from -5 to 5
- draft_values: bfloat16 [512, 2048], P('seq', 'tensor'), may hold values from -6 to 6
- key_cache: bfloat16 [96, 128, 2048], P('seq', None, 'tensor'), may hold values from -6 to 6
- value_cache: bfloat16 [96, 128, 2048], P('seq', None, 'tensor'), may hold values from -6 to 6
- page_request: int32 [96], P('seq'), may hold values from 0 to 7, as said below
- page_slot: int32 [96], P('seq'), may hold values from 0 to 88, as said below
- cache_len: int32 [8], replicated, may hold values from 1 to 11384, as said below
- tree_mask: int32 [8, 64, 64], P('seq'), may hold values from 0 to 1, as said below
- accepted: int32 [8, 8], P('seq'), may hold values from 0 to 28, as said below
- hidden_in: bfloat16 [512, 2048], P('seq'), may hold values from -0.75 to 0.75
- out_proj: bfloat16 [2048, 2048], P('tensor'), may hold values from -0.125 to 0.125
- norm_gain: float32 [2048], replicated, may hold values from 0.5 to 1.5
- gate_proj: bfloat16 [64, 2048, 1024], P('seq', None, 'tensor'), may hold values from -0.125 to 0.125
- up_proj: bfloat16 [64, 2048, 1024], P('seq', None, 'tensor'), may hold values from -0.125 to 0.125
- down_proj: bfloat16 [64, 1024, 2048], P('seq', 'tensor'), may hold values from -0.1875 to 0.1875
- expert_ids: int32 [512, 8], P('seq'), may hold values from 0 to 63, all different within a row; in each aligned block of 64 rows (0 to 63, 64 to 127, ...) at most 16 rows name the same one
- route_weight: float32 [512, 8], P('seq'), may hold values from 0.02 to 0.5
Outputs:
- mixed_out: bfloat16 [512, 2048], P('seq', 'tensor')
- log_sum_exp: float32 [512, 16], P('seq', 'tensor')
- key_cache_out: bfloat16 [96, 128, 2048], P('seq', None, 'tensor')
- value_cache_out: bfloat16 [96, 128, 2048], P('seq', None, 'tensor')
The draws below stay inside these ranges and needn't reach their ends.
Inputs may be any that keep to these rules, and one draw needn't show every extreme that they name: `page_request`: every request holds one or more pages and at most 128; together they hold all 96 pages, and one request holds min(128, 89). `page_slot`: the pages of one request carry the numbers 0, 1, 2 and so on, each once. A request's pages hold cache_len + 8 positions or more, and its last page holds at least one of its first cache_len positions. `tree_mask`: row i marks node i and its ancestors in a tree rooted at node 0; each node's parent stands one to four nodes before it. `accepted`: the 8 nodes nearest the root on a path from node 0, in order from the root. `expert_ids`: at most 16 of the 64 rows of one request name the same expert.
All inputs are finite; a program needn't handle non-finite values.
Results may differ from the reference program's by a relative error of at most 0.024.
Values may be sent and summed in bfloat16 or wider, within the bound.
No kernel may reach another device: no remote copies, remote signals or barrier semaphores. Data moves between devices by JAX's collectives and lax.ppermute only.
A program may use at most 128 MiB of HBM per device.

```python
import math
import jax
import jax.numpy as jnp
import numpy as np
from jax import lax

D = 2048
HEADS = 16
HD = 128
EXPERTS = 64
FFE = 1024
TOPK = 8
DRAFT = 64
ACC = 8
PAGE = 128
MAXP = 128
REQS = 8
TOKENS = 512
POOL = 96
CAP = 16
N_SEQ = 8
N_TENSOR = 4


def layout_pages(key):
    most_pages = min(MAXP, POOL - REQS + 1)
    extra = POOL - most_pages - (REQS - 1)
    draws = max(extra, 1)
    keys = jax.random.split(jax.random.fold_in(key, 11), 5)
    longest = jax.random.randint(keys[0], (), 0, REQS)
    first_pick = jax.random.randint(keys[1], (draws,), 0, max(REQS - 1, 1))
    second_pick = jax.random.randint(keys[2], (draws,), 0, max(REQS - 1, 1))
    chosen = first_pick * second_pick // max(REQS - 1, 1)
    counted = (jnp.arange(draws)[:, None] < extra) & (chosen[:, None] == jnp.arange(max(REQS - 1, 1))[None, :])
    others = 1 + jnp.sum(counted.astype(jnp.int32), axis=0)
    request_ids = jnp.arange(REQS)
    other_index = jnp.clip(request_ids - (request_ids > longest).astype(jnp.int32), 0, max(REQS - 2, 0))
    counts = jnp.where(request_ids == longest, most_pages, others[other_index]).astype(jnp.int32)
    ends = jnp.cumsum(counts)
    starts = ends - counts
    order = jnp.arange(POOL)
    holder = jnp.sum((order[:, None] >= ends[None, :]).astype(jnp.int32), axis=1)
    number = order - starts[holder]
    shuffle = jax.random.permutation(keys[3], POOL)
    page_request = jnp.zeros((POOL,), jnp.int32).at[shuffle].set(holder.astype(jnp.int32))
    page_slot = jnp.zeros((POOL,), jnp.int32).at[shuffle].set(number.astype(jnp.int32))
    slack = jax.random.randint(keys[4], (REQS,), 0, PAGE - ACC)
    slack = jnp.where(request_ids == longest, 0, slack)
    cache_len = (counts * PAGE - ACC - slack).astype(jnp.int32)
    return (page_request, page_slot, cache_len)


def tree_layout(key):
    keys = jax.random.split(jax.random.fold_in(key, 23), 3)
    nodes = jnp.arange(DRAFT)
    request_ids = jnp.arange(REQS)
    forced = jax.random.randint(keys[2], (), 0, REQS)
    is_forced = request_ids == forced
    stride = jax.random.randint(keys[0], (REQS, DRAFT), 1, 5)
    stride = jnp.where(is_forced[:, None], 4, stride)
    parent = jnp.maximum(nodes[None, :] - jnp.minimum(stride, jnp.maximum(nodes, 1)[None, :]), 0)
    identity = (nodes[:, None] == nodes[None, :]).astype(jnp.int32)
    start_mask = jnp.broadcast_to(identity, (REQS, DRAFT, DRAFT))

    def add_node(index, mask_now):
        parent_now = lax.dynamic_slice_in_dim(parent, index, 1, 1)[:, 0]
        parent_row = jnp.take_along_axis(mask_now, jnp.broadcast_to(parent_now[:, None, None], (REQS, 1, DRAFT)), axis=1)
        own_row = lax.dynamic_slice_in_dim(identity, index, 1, 0)[None]
        return lax.dynamic_update_slice_in_dim(mask_now, jnp.maximum(parent_row, own_row), index, 1)
    tree_mask = lax.fori_loop(1, DRAFT, add_node, start_mask)
    target = jax.random.randint(keys[1], (REQS,), DRAFT // 2, DRAFT)
    target = jnp.where(is_forced, (DRAFT - 1) // 4 * 4, target)
    path_row = jnp.take_along_axis(tree_mask, jnp.broadcast_to(target[:, None, None], (REQS, 1, DRAFT)), axis=1)[:, 0, :]
    running = jnp.cumsum(path_row, axis=1)
    accepted = jnp.sum((running[:, None, :] < (jnp.arange(ACC) + 1)[None, :, None]).astype(jnp.int32), axis=2)
    return (tree_mask.astype(jnp.int32), accepted.astype(jnp.int32))


def draw_page_request(key, part):
    return layout_pages(key)[0]


def draw_page_slot(key, part):
    return layout_pages(key)[1]


def draw_cache_len(key, part):
    return layout_pages(key)[2]


def draw_tree_mask(key, part):
    return tree_layout(key)[0]


def draw_accepted(key, part):
    return tree_layout(key)[1]


def draw_queries(key, part):
    base = jnp.clip(jax.random.normal(jax.random.fold_in(key, 41), (TOKENS, HEADS * HD), jnp.float32), -4.0, 4.0)
    return base.astype(jnp.bfloat16)


def draw_draft_keys(key, part):
    base = jnp.clip(jax.random.normal(jax.random.fold_in(key, 43), (TOKENS, HEADS * HD), jnp.float32), -4.0, 4.0)
    return base.astype(jnp.bfloat16)


def shard_levels(stream_key, dims, pieces, low, top_value):
    loudness, own = 1.0, jax.random.fold_in(stream_key, 6)
    for dim, parts in pieces:
        steps = jnp.exp(jax.random.uniform(jax.random.fold_in(own, dim), (parts,), jnp.float32, low / len(pieces), top_value / len(pieces)))
        loudness = loudness * jnp.repeat(steps, dims[dim] // parts).reshape([-1 if axis == dim else 1 for axis in range(len(dims))])
    return loudness


def routed_block(rng, own, number, rows, number_of, top, limit, lean):
    sequence = jax.random.permutation(rng, number_of)
    crowded, usual = shares(number_of, rows * top, limit, lean, True), shares(number_of, rows * top, limit, lean, False)
    places = jnp.arange(number_of)

    def named(lengths, offset_by):
        used = int((lengths > 0).sum())
        fixed = max(1, used // 4)
        passed = fixed + (places - fixed + offset_by * (used - fixed)) % max(1, number_of - fixed)
        return jnp.zeros((number_of,), jnp.int32).at[sequence[jnp.where(places < fixed, places, passed)]].set(jnp.asarray(lengths, jnp.int32))

    lengths = jnp.where(number % 4 == 0, named(crowded, number // 4), named(usual, number - number // 4 - 1))
    mixed = jax.random.permutation(jax.random.fold_in(own, 3), number_of)
    giver, taker = mixed[0:number_of // 2 * 2:2], mixed[1:number_of // 2 * 2:2]
    margin = jnp.minimum(lengths[giver] - 1, limit - lengths[taker]) // 2
    margin = jnp.where((giver == sequence[0]) | (taker == sequence[0]) | (lengths[taker] == 0), 0, jnp.maximum(margin, 0))
    passed = jax.random.randint(jax.random.fold_in(own, 4), (number_of // 2,), 0, 1 << 20) % (margin + 1)
    lengths = lengths.at[giver].add(-passed).at[taker].add(passed)
    items = jnp.searchsorted(jnp.cumsum(lengths), jnp.arange(rows * top), side="right").astype(jnp.int32)
    grid = items.reshape(top, rows).T
    grid = grid[jax.random.permutation(jax.random.fold_in(own, 1), rows)]
    offset_by = jax.random.randint(jax.random.fold_in(own, 2), (rows, 1), 0, top)
    return jnp.take_along_axis(grid, (jnp.arange(top)[None, :] + offset_by) % top, axis=1)


def shares(number_of, total, most, skew, full):
    portions = [(1 << 20) // math.isqrt(grade ** skew) + 1 for grade in range(1, number_of + 1)]
    largest = most if full else min(most, max(-(-total // number_of), total * portions[0] // sum(portions)))
    least = 1 if total - largest >= number_of - 1 else 0
    given, surplus = [largest] + [least] * (number_of - 1), total - largest - least * (number_of - 1)
    while surplus > 0:
        movable = [i for i in range(1, number_of) if given[i] < largest] or [i for i in range(1, number_of) if given[i] < most]
        pool, remaining = sum([portions[i] for i in movable]), surplus
        for i in movable:
            more = min(most - given[i], max(1, remaining * portions[i] // pool), surplus)
            given[i] = given[i] + more
            surplus = surplus - more
    return np.array(given)


def noise(rng, shape, scale, limit, shards=(), kind=jnp.bfloat16):
    result = scale * jax.random.normal(rng, shape, jnp.float32)
    if shards:
        result = result * shard_levels(rng, shape, shards, -0.22, 0.18)
    return jnp.clip(result, -limit, limit).astype(kind)


def setup_inputs(seed: int = 0) -> dict:
    key_of = jax.random.split(jax.random.key(seed), 19)
    queries = draw_queries(jax.random.fold_in(key_of[18], 71), 0)
    draft_keys = draw_draft_keys(jax.random.fold_in(key_of[18], 71), 0)
    draft_values = noise(key_of[2], (TOKENS, HEADS * HD), 1.0, 6.0, ((0, 8), (1, 4)))
    key_cache = noise(key_of[3], (POOL, PAGE, HEADS * HD), 1.0, 6.0, ((0, 8), (2, 4)))
    value_cache = noise(key_of[4], (POOL, PAGE, HEADS * HD), 1.0, 6.0, ((0, 8), (2, 4)))
    page_request = draw_page_request(jax.random.fold_in(key_of[18], 71), 0)
    page_slot = draw_page_slot(jax.random.fold_in(key_of[18], 71), 0)
    cache_len = draw_cache_len(jax.random.fold_in(key_of[18], 71), 0)
    tree_mask = draw_tree_mask(jax.random.fold_in(key_of[18], 71), 0)
    accepted = draw_accepted(jax.random.fold_in(key_of[18], 71), 0)
    hidden_in = noise(key_of[10], (TOKENS, D), 0.05, 0.75, ((0, 8),))
    out_proj = noise(key_of[11], (HEADS * HD, D), (HEADS * HD) ** -0.5, 0.125, ((0, 4),))
    norm_gain = jnp.clip(1.0 + 0.1 * jax.random.normal(key_of[12], (D,), jnp.float32), 0.5, 1.5)
    gate_proj = noise(key_of[13], (EXPERTS, D, FFE), D ** -0.5, 0.125, ((0, 8), (2, 4)))
    up_proj = noise(key_of[14], (EXPERTS, D, FFE), D ** -0.5, 0.125, ((0, 8), (2, 4)))
    down_proj = noise(key_of[15], (EXPERTS, FFE, D), FFE ** -0.5, 0.1875, ((0, 8), (1, 4)))
    expert_ids_keys = jax.random.split(jax.random.fold_in(key_of[16], 1), TOKENS // DRAFT)
    expert_ids_turns = jax.random.permutation(jax.random.fold_in(key_of[16], 3), TOKENS // DRAFT)
    expert_ids = jax.vmap(lambda own, number: routed_block(jax.random.fold_in(key_of[16], 2), own, number, DRAFT, EXPERTS, TOPK, CAP, 2))(expert_ids_keys, expert_ids_turns).reshape((TOKENS, TOPK))
    route_weight = jnp.clip(jnp.exp(math.log(0.5) - 3.218876 * jax.random.uniform(key_of[17], (TOKENS, TOPK), jnp.float32) ** shard_levels(key_of[17], (TOKENS, TOPK), ((0, 8),), -0.2, 0.2)), 0.02, 0.5)
    return dict(queries=queries, draft_keys=draft_keys, draft_values=draft_values, key_cache=key_cache, value_cache=value_cache, page_request=page_request, page_slot=page_slot, cache_len=cache_len, tree_mask=tree_mask, accepted=accepted, hidden_in=hidden_in, out_proj=out_proj, norm_gain=norm_gain, gate_proj=gate_proj, up_proj=up_proj, down_proj=down_proj, expert_ids=expert_ids, route_weight=route_weight)


MASKED = -1e+30

def reference(queries, draft_keys, draft_values, key_cache, value_cache, page_request, page_slot, cache_len, tree_mask, accepted, hidden_in, out_proj, norm_gain, gate_proj, up_proj, down_proj, expert_ids, route_weight):
    head_width = HEADS * HD
    page_table = jnp.zeros((REQS, MAXP), jnp.int32).at[page_request, page_slot].set(jnp.arange(POOL, dtype=jnp.int32))
    scaling = 1.0 / math.sqrt(HD)
    cache_span = jnp.arange(MAXP * PAGE, dtype=jnp.int32)

    def per_request(request):
        table_row = page_table[request]
        far_keys = key_cache[table_row].reshape(MAXP * PAGE, HEADS, HD).astype(jnp.float32)
        far_values = value_cache[table_row].reshape(MAXP * PAGE, HEADS, HD).astype(jnp.float32)
        first_row = (request * DRAFT).astype(jnp.int32)
        own_queries = lax.dynamic_slice_in_dim(queries, first_row, DRAFT, 0).reshape(DRAFT, HEADS, HD).astype(jnp.float32)
        own_keys = lax.dynamic_slice_in_dim(draft_keys, first_row, DRAFT, 0).reshape(DRAFT, HEADS, HD).astype(jnp.float32)
        own_values = lax.dynamic_slice_in_dim(draft_values, first_row, DRAFT, 0).reshape(DRAFT, HEADS, HD).astype(jnp.float32)
        far_scores = jnp.einsum('qhd,khd->hqk', own_queries, far_keys) * scaling
        far_scores = jnp.where((cache_span < cache_len[request])[None, None, :], far_scores, MASKED)
        near_scores = jnp.einsum('qhd,khd->hqk', own_queries, own_keys) * scaling
        near_scores = jnp.where((tree_mask[request] > 0)[None], near_scores, MASKED)
        scores = jnp.concatenate([far_scores, near_scores], axis=2)
        row_max = lax.optimization_barrier(jnp.max(scores, axis=2))
        weights = jnp.exp(scores - row_max[:, :, None])
        total_sum = lax.optimization_barrier(jnp.sum(weights, axis=2))
        probs = lax.optimization_barrier(weights.astype(jnp.bfloat16)).astype(jnp.float32)
        all_values = jnp.concatenate([far_values, own_values], axis=0)
        summed = jnp.einsum('hqk,khd->hqd', probs, all_values)
        attended = (summed / total_sum[:, :, None]).transpose(1, 0, 2).reshape(DRAFT, head_width).astype(jnp.bfloat16)
        return (attended, (row_max + jnp.log(total_sum)).T)
    attended, log_rows = lax.map(per_request, jnp.arange(REQS, dtype=jnp.int32))
    attended = attended.reshape(TOKENS, head_width)
    log_sum_exp = log_rows.reshape(TOKENS, HEADS)
    mixed = hidden_in.astype(jnp.float32) + jnp.dot(attended, out_proj, preferred_element_type=jnp.float32)
    normed = (mixed * lax.rsqrt(lax.optimization_barrier(jnp.mean(mixed * mixed, axis=1, keepdims=True)) + 1e-06) * norm_gain).astype(jnp.bfloat16)
    row_limit = CAP * N_SEQ
    block_width = FFE // N_TENSOR

    def per_expert(running, expert):
        matches = expert_ids == expert
        picked = jnp.any(matches, axis=1)
        share_weight = lax.optimization_barrier(jnp.sum(jnp.where(matches, route_weight, 0.0), axis=1))
        chosen = jnp.nonzero(picked, size=row_limit, fill_value=0)[0].astype(jnp.int32)
        inputs = normed[chosen]
        gate_value = jnp.dot(inputs, gate_proj[expert], preferred_element_type=jnp.float32)
        up_value = jnp.dot(inputs, up_proj[expert], preferred_element_type=jnp.float32)
        active = (jax.nn.silu(gate_value) * up_value).astype(jnp.bfloat16)
        output = jnp.zeros((row_limit, D), jnp.float32)
        for quarter in range(N_TENSOR):
            partial_value = jnp.dot(active[:, quarter * block_width:(quarter + 1) * block_width], down_proj[expert, quarter * block_width:(quarter + 1) * block_width], preferred_element_type=jnp.float32)
            output = output + lax.optimization_barrier(partial_value.astype(jnp.bfloat16)).astype(jnp.float32)
        is_valid = jnp.arange(row_limit, dtype=jnp.int32) < jnp.sum(picked.astype(jnp.int32))
        factor = jnp.where(is_valid, share_weight[chosen], 0.0)
        return (running.at[chosen].add(factor[:, None] * output), None)
    moe, _ = lax.scan(per_expert, jnp.zeros((TOKENS, D), jnp.float32), jnp.arange(EXPERTS, dtype=jnp.int32))
    mixed_out = (mixed + moe).astype(jnp.bfloat16)
    offsets = jnp.arange(ACC, dtype=jnp.int32)
    positions = (cache_len[:, None] + offsets[None, :]).astype(jnp.int32)
    target_page = jnp.take_along_axis(page_table, positions // PAGE, axis=1)
    target_cell = positions % PAGE
    source_rows = (jnp.arange(REQS, dtype=jnp.int32)[:, None] * DRAFT + accepted).astype(jnp.int32)
    key_cache_out = key_cache.at[target_page, target_cell].set(draft_keys[source_rows])
    value_cache_out = value_cache.at[target_page, target_cell].set(draft_values[source_rows])
    return (mixed_out, log_sum_exp, key_cache_out, value_cache_out)
```

```python
import functools
import math

import jax
import jax.numpy as jnp
from jax import lax
from jax.experimental import pallas as pl
from jax.experimental.pallas import tpu as pltpu
from jax.sharding import PartitionSpec as P

HD = 128
CAP = 16
MASKED = -1e30
F32 = jnp.float32
BF16 = jnp.bfloat16
I32 = jnp.int32
STAT = 128
VMEM_LIMIT = 56 * 1024 * 1024


def vmem():
    return pl.BlockSpec(memory_space=pltpu.VMEM)


def smem():
    return pl.BlockSpec(memory_space=pltpu.SMEM)


def shape(dims, dtype):
    return jax.ShapeDtypeStruct(dims, dtype)


def params():
    return pltpu.CompilerParams(vmem_limit_bytes=VMEM_LIMIT)


def cost(flops, moved):
    return pl.CostEstimate(flops=flops, bytes_accessed=moved, transcendentals=0)


def each(count, body):
    if count <= 16:
        for i in range(count):
            body(i)
    else:

        @pl.loop(0, count)
        def _(i):
            body(i)


def dot(a, b):
    return jnp.dot(a, b, preferred_element_type=F32)


def dot_t(a, b):
    return lax.dot_general(a, b, (((1,), (1,)), ((), ())), preferred_element_type=F32)


def aligned(index, size):
    return index * size if isinstance(index, int) else pl.multiple_of(index * size, size)


def three_parts(value):
    high = value.astype(BF16).astype(F32)
    rest = value - high
    middle = rest.astype(BF16).astype(F32)
    return high, middle, rest - middle


def near_kernel(q_ref, k_ref, v_ref, mask_ref, acc_ref, ids_ref, rw_ref, out_ref, lse_ref, pack_ref):
    draft, width = q_ref.shape
    scaling = 1.0 / math.sqrt(HD)
    seen = mask_ref[0] > 0
    for h in range(width // HD):
        cols = slice(h * HD, (h + 1) * HD)
        scores = jnp.where(seen, dot_t(q_ref[:, cols], k_ref[:, cols]) * scaling, MASKED)
        top = jnp.max(scores, axis=1, keepdims=True)
        weights = jnp.exp(scores - top)
        total = jnp.sum(weights, axis=1, keepdims=True)
        out_ref[:, cols] = dot(weights.astype(BF16), v_ref[:, cols]) / total
        lse_ref[:, cols] = jnp.broadcast_to(top + jnp.log(total), (draft, HD))
    accepted = acc_ref.shape[0]
    pick = (lax.broadcasted_iota(I32, (accepted, draft), 1) == acc_ref[...]).astype(F32).astype(BF16)
    rows = jnp.concatenate([dot(pick, k_ref[...]), dot(pick, v_ref[...])], axis=0)
    pack_ref[0, 0 : 2 * accepted, :] = rows.astype(BF16)
    pack_ref[0, 2 * accepted :, :] = jnp.zeros((16, width), BF16)
    zero = jnp.zeros((8, draft), F32)
    for g, part in enumerate((ids_ref[...], *three_parts(rw_ref[...]))):
        pack_ref[0, 2 * accepted :, g * 128 : g * 128 + draft] = jnp.concatenate([part, zero], axis=0).astype(BF16)


def far_kernel(pos_ref, live_ref, key_ref, value_ref, *refs, counts, n_out):
    pieces, outs = refs[: len(counts)], refs[len(counts) : len(counts) + n_out]
    q_s, m_s, l_s, o_s = refs[len(counts) + n_out :]
    pages, page_len, width = key_ref.shape
    draft = q_s.shape[1]
    heads = width // HD
    scaling = 1.0 / math.sqrt(HD)
    at = 0
    for piece, count in zip(pieces, counts):
        q_s[at : at + count] = piece[...]
        at += count

    def clear(i):
        m_s[i] = jnp.full((draft, width), MASKED, F32)
        l_s[i] = jnp.zeros((draft, width), F32)
        o_s[i] = jnp.zeros((draft, width), F32)

    each(at, clear)
    cell = lax.broadcasted_iota(I32, (draft, page_len), 1)
    for p in range(pages):
        pos = pos_ref[p]
        alive = cell < live_ref[p]
        for h in range(heads):
            cols = slice(h * HD, (h + 1) * HD)
            scores = dot_t(q_s[pos, :, cols], key_ref[p, :, cols]) * scaling
            scores = jnp.where(alive, scores, MASKED)
            top = jnp.max(scores, axis=1, keepdims=True)
            weights = jnp.exp(scores - top)
            total = jnp.sum(weights, axis=1, keepdims=True)
            out = dot(weights.astype(BF16), value_ref[p, :, cols])
            old = m_s[pos, :, cols]
            new = jnp.maximum(old, top)
            keep, add = jnp.exp(old - new), jnp.exp(top - new)
            m_s[pos, :, cols] = new
            l_s[pos, :, cols] = l_s[pos, :, cols] * keep + total * add
            o_s[pos, :, cols] = o_s[pos, :, cols] * keep + out * add
    lane = lax.broadcasted_iota(I32, (draft, STAT), 1)

    def finish(i):
        target, row = (outs[i], 0) if n_out > 1 else (outs[0], i)
        stat = jnp.zeros((draft, STAT), F32)
        for h in range(heads):
            cols = slice(h * HD, (h + 1) * HD)
            total = l_s[i, :, cols]
            some = total > 0.0
            safe = jnp.where(some, total, 1.0)
            target[row, :, cols] = (o_s[i, :, cols] / safe).astype(BF16)
            lse = jnp.where(some, m_s[i, :, cols] + jnp.log(safe), MASKED)
            stat = jnp.where(lane % heads == h, lse, stat)
        high, middle, low = three_parts(stat)
        packed = jnp.where(lane < heads, high, jnp.where(lane < 2 * heads, middle, low))
        target[row, :, width:] = packed.astype(BF16)

    each(at, finish)


def merge_kernel(t_ref, near_ref, lse_ref, hidden_ref, w_ref, *refs, counts, n_out):
    pieces, refs = refs[: len(counts)], refs[len(counts) :]
    lse_out, outs = refs[0], refs[1:]
    draft, width = near_ref.shape
    heads = width // HD
    rows = [(piece, i) for piece, count in zip(pieces, counts) for i in range(count)]
    stats = [piece[i, :, width:].astype(F32) for piece, i in rows]
    attended = []
    for h in range(heads):
        cols = slice(h * HD, (h + 1) * HD)
        sums = [
            s[:, h : h + 1] + s[:, heads + h : heads + h + 1] + s[:, 2 * heads + h : 2 * heads + h + 1]
            for s in stats
        ]
        own = lse_ref[:, h * HD : h * HD + 1]
        top = functools.reduce(jnp.maximum, sums, own)
        weight = jnp.exp(own - top)
        total = weight
        summed = near_ref[:, cols] * weight
        for (piece, i), s in zip(rows, sums):
            weight = jnp.exp(s - top)
            total = total + weight
            summed = summed + piece[i, :, cols].astype(F32) * weight
        attended.append((summed / total).astype(BF16))
        lse_out[:, h : h + 1] = top + jnp.log(total)
    attended = jnp.concatenate(attended, axis=1)
    if n_out == 1:
        outs[0][...] = dot(attended, w_ref[...]).astype(outs[0].dtype)
        return
    for n in range(n_out):
        start = pl.multiple_of((t_ref[0] ^ n) * width, width)
        part = dot(attended, w_ref[:, pl.ds(start, width)])
        if n == 0:
            part = part + hidden_ref[:, pl.ds(start, width)].astype(F32)
        outs[n][...] = part.astype(outs[n].dtype)


def slots_kernel(me_ref, *refs, counts, experts, accept):
    pieces, (g_ref, c_ref, w_ref) = refs[: len(counts)], refs[len(counts) :]
    draft = g_ref.shape[2]
    upper = (
        lax.broadcasted_iota(I32, (draft, draft), 0) < lax.broadcasted_iota(I32, (draft, draft), 1)
    ).astype(F32).astype(BF16)
    same = (
        lax.broadcasted_iota(I32, (draft, draft), 0) == lax.broadcasted_iota(I32, (draft, draft), 1)
    ).astype(F32).astype(BF16)
    number = lax.broadcasted_iota(I32, (CAP, draft), 0).astype(F32)
    first = me_ref[0] * experts

    def one(piece, i, m):
        def part(g):
            return piece[i, 2 * accept : 2 * accept + 16, g * 128 : g * 128 + draft].astype(F32)[0:8]

        ids, weight = part(0), part(1) + part(2) + part(3)
        hits, weights = [], []
        for e in range(experts):
            hit = ids == (first + e).astype(F32)
            hits.append(jnp.max(jnp.where(hit, 1.0, 0.0), axis=0, keepdims=True))
            weights.append(jnp.sum(jnp.where(hit, weight, 0.0), axis=0, keepdims=True))
        table = jnp.concatenate(hits + [jnp.zeros((16 - experts, draft), F32)], axis=0)
        rank = dot(table.astype(BF16), upper)
        blocks = []
        for e in range(experts):
            block = jnp.where((number == rank[e : e + 1]) & (hits[e] > 0.0), 1.0, 0.0)
            blocks.append(block)
            row_weight = jnp.sum(block * weights[e], axis=1, keepdims=True)
            w_ref[e, pl.ds(aligned(m, CAP), CAP), :] = jnp.broadcast_to(row_weight, (CAP, 128))
        stacked = jnp.concatenate(blocks, axis=0).astype(BF16)
        g_ref[m] = stacked
        c_ref[m] = dot_t(same, stacked).astype(BF16)

    if len(counts) > 1:
        for m, piece in enumerate(pieces):
            one(piece, 0, m)
    else:
        each(counts[0], lambda m: one(pieces[0], m, m))


def cache_kernel(pos_ref, live_ref, key_ref, value_ref, *refs, counts, accept):
    pieces, (key_out, value_out, table) = refs[: len(counts)], refs[len(counts) :]
    page_len, width = key_ref.shape[1:]
    p = pl.program_id(0)

    @pl.when(p == 0)
    def _():
        at = 0
        for piece, count in zip(pieces, counts):
            table[at : at + count] = piece[:, 0 : 2 * accept, :]
            at += count

    live = live_ref[p]
    reached = (live > -accept) & (live < page_len)

    @pl.when(jnp.logical_not(reached))
    def _():
        key_out[...] = key_ref[...]
        value_out[...] = value_ref[...]

    @pl.when(reached)
    def _():
        rows = table[pos_ref[p]]
        offset = lax.broadcasted_iota(I32, (page_len, 2 * accept), 0) - live
        column = lax.broadcasted_iota(I32, (page_len, 2 * accept), 1)
        cell = lax.broadcasted_iota(I32, (page_len, width), 0) - live
        touched = (cell >= 0) & (cell < accept)
        for source, out, shift in ((key_ref, key_out, 0), (value_ref, value_out, accept)):
            hit = (offset == column - shift) & (offset >= 0) & (offset < accept)
            place = jnp.where(hit, 1.0, 0.0).astype(BF16)
            out[0] = jnp.where(touched, dot(place, rows), source[0].astype(F32)).astype(BF16)


def expert_kernel(t_ref, gain_ref, g_ref, rw_ref, gate_ref, up_ref, *refs, layout):
    pieces, (out_ref, xs) = refs[:-2], refs[-2:]
    e = pl.program_id(0)
    experts, slots, model = xs.shape
    draft = g_ref.shape[2]

    @pl.when(e == 0)
    def _():
        gain = gain_ref[...]

        def one(m):
            parts = layout(pieces, m)
            square = sum(jnp.sum(v * v, axis=1, keepdims=True) for _, v in parts)
            scale = lax.rsqrt(square / model + 1e-6)
            for n, v in parts:
                width = v.shape[1]
                if n is None:
                    cols, sub_gain = slice(0, width), gain
                else:
                    cols = pl.ds(pl.multiple_of((t_ref[0] ^ n) * width, width), width)
                    sub_gain = gain_ref[:, cols]
                normed = (v * scale * sub_gain).astype(BF16)
                picked = dot(g_ref[m], normed).astype(BF16)
                for i in range(experts):
                    xs[i, pl.ds(aligned(m, CAP), CAP), cols] = picked[i * CAP : (i + 1) * CAP]

        each(g_ref.shape[0], one)

    rows = xs[e]
    gate = dot(rows, gate_ref[0])
    up = dot(rows, up_ref[0])
    active = gate / (1.0 + jnp.exp(-gate)) * up
    out_ref[0] = (active * rw_ref[0, :, 0:1]).astype(BF16)


def down_kernel(cols_ref, active_ref, c_ref, down_ref, out_ref, y_s):
    experts, slots, _ = active_ref.shape
    groups, draft = c_ref.shape[0:2]
    for e in range(experts):
        y_s[e] = dot(active_ref[e], down_ref[e]).astype(BF16)

    def one(m):
        rows = pl.ds(aligned(m, CAP), CAP)
        block = jnp.concatenate([y_s[e, rows, :] for e in range(experts)], axis=0)
        out_ref[0, m] = dot(c_ref[m], block).astype(BF16)

    each(groups, one)


def add_kernel(*refs, body, n_in):
    body(refs[:n_in], refs[n_in:])


def small(body, ins, outs):
    return pl.pallas_call(
        functools.partial(add_kernel, body=body, n_in=len(ins)),
        out_shape=outs,
        in_specs=[vmem()] * len(ins),
        out_specs=[vmem()] * len(outs),
        compiler_params=params(),
    )(*ins)


def on_device(
    queries,
    draft_keys,
    draft_values,
    key_cache,
    value_cache,
    page_request,
    page_slot,
    cache_len,
    tree_mask,
    accepted,
    hidden_in,
    out_proj,
    norm_gain,
    gate_proj,
    up_proj,
    down_proj,
    expert_ids,
    route_weight,
):
    draft, width = queries.shape
    pages, page_len, _ = key_cache.shape
    model = hidden_in.shape[1]
    heads = width // HD
    seq, tensor = lax.axis_size("seq"), lax.axis_size("tensor")
    experts = gate_proj.shape[0]
    hidden = gate_proj.shape[2]
    accept = accepted.shape[1]
    slots = seq * CAP
    staged = seq == 8 and tensor == 4
    me, t = lax.axis_index("seq"), lax.axis_index("tensor")

    def hop(axis, mask):
        size = seq if axis == "seq" else tensor
        pairs = [(i, i ^ mask) for i in range(size)]
        return lambda v: lax.ppermute(v, axis, pairs)

    x1, y1, core = hop("seq", 1), hop("tensor", 2), hop("tensor", 1)
    zs = [hop("seq", 2 * k) for k in (1, 2, 3)]

    def gather_seq(v):
        if not staged:
            return [lax.all_gather(v, "seq", axis=0, tiled=True)]
        beside = x1(v)
        line = [z(v) for z in zs]
        return [v, *line, beside, *[x1(b) for b in line]]

    relative = page_request ^ me if staged else page_request
    pos = (relative & 1) * 4 + (relative >> 1) if staged else relative
    pos = pos.astype(I32)
    request_hit = page_request[:, None] == jnp.arange(cache_len.shape[0], dtype=I32)[None, :]
    live = jnp.sum(jnp.where(request_hit, cache_len[None, :], 0), axis=1) - page_slot * page_len
    me1, t1 = me.reshape(1).astype(I32), t.reshape(1).astype(I32)

    every_query = gather_seq(queries[None])
    counts = tuple(a.shape[0] for a in every_query)

    near_out, near_lse, pack = pl.pallas_call(
        near_kernel,
        out_shape=[
            shape((draft, width), F32),
            shape((draft, width), F32),
            shape((1, 2 * accept + 16, width), BF16),
        ],
        in_specs=[vmem()] * 7,
        out_specs=[vmem()] * 3,
        compiler_params=params(),
        name="near",
    )(
        queries,
        draft_keys,
        draft_values,
        tree_mask,
        accepted.reshape(accept, 1),
        expert_ids.T.astype(F32),
        route_weight.T,
    )

    n_out = seq if staged else 1
    partials = pl.pallas_call(
        functools.partial(far_kernel, counts=counts, n_out=n_out),
        out_shape=[shape((seq // n_out, draft, width + STAT), BF16)] * n_out,
        in_specs=[smem(), smem()] + [vmem()] * (2 + len(every_query)),
        out_specs=[vmem()] * n_out,
        scratch_shapes=[
            pltpu.VMEM((seq, draft, width), BF16),
            pltpu.VMEM((seq, draft, width), F32),
            pltpu.VMEM((seq, draft, width), F32),
            pltpu.VMEM((seq, draft, width), F32),
        ],
        compiler_params=params(),
        name="far",
    )(pos, live, key_cache, value_cache, *every_query)

    every_pack = gather_seq(pack)

    if staged:
        back = [partials[0]]
        for place in range(1, 8):
            back.append(hop("seq", (place & 3) * 2 + (place >> 2))(partials[place]))
    else:
        back = [lax.all_to_all(partials[0], "seq", split_axis=0, concat_axis=0, tiled=True)]

    n_parts = tensor if staged else 1
    part_shape = (
        [shape((draft, width), F32)] + [shape((draft, width), BF16)] * 3 if staged else [shape((draft, model), F32)]
    )
    log_sum_exp, *parts = pl.pallas_call(
        functools.partial(merge_kernel, counts=tuple(b.shape[0] for b in back), n_out=n_parts),
        out_shape=[shape((draft, heads), F32)] + part_shape,
        in_specs=[smem()] + [vmem()] * (4 + len(back)),
        out_specs=[vmem()] * (1 + n_parts),
        compiler_params=params(),
        name="merge",
    )(t1, near_out, near_lse, hidden_in, out_proj, *back)

    if staged:
        got = [hop("tensor", n)(parts[n]) for n in (1, 2, 3)]
        mixed = parts[0] + got[0].astype(F32) + got[1].astype(F32) + got[2].astype(F32)
    else:
        summed = lax.psum(parts[0], "tensor") + hidden_in.astype(F32)
        mixed = lax.dynamic_slice_in_dim(summed, t * width, width, 1)
    row = mixed.astype(BF16)[None]

    grouped, combine, slot_weight = pl.pallas_call(
        functools.partial(
            slots_kernel, counts=tuple(a.shape[0] for a in every_pack), experts=experts, accept=accept
        ),
        out_shape=[
            shape((seq, experts * CAP, draft), BF16),
            shape((seq, draft, experts * CAP), BF16),
            shape((experts, slots, 128), F32),
        ],
        in_specs=[smem()] + [vmem()] * len(every_pack),
        out_specs=[vmem()] * 3,
        compiler_params=params(),
        name="slots",
    )(me1, *every_pack)

    page_spec = pl.BlockSpec((1, page_len, width), lambda p: (p, 0, 0))
    key_cache_out, value_cache_out = pl.pallas_call(
        functools.partial(cache_kernel, counts=tuple(a.shape[0] for a in every_pack), accept=accept),
        grid=(pages,),
        out_shape=[shape(key_cache.shape, BF16), shape(value_cache.shape, BF16)],
        in_specs=[smem(), smem(), page_spec, page_spec] + [vmem()] * len(every_pack),
        out_specs=[page_spec, page_spec],
        scratch_shapes=[pltpu.VMEM((seq, 2 * accept, width), BF16)],
        compiler_params=params(),
        name="cache",
    )(pos, live, key_cache, value_cache, *every_pack)

    if staged:
        line = [row] + [z(row) for z in zs]
        line = [jnp.concatenate(line[0:2]), jnp.concatenate(line[2:4])]
        over_x, over_y = [x1(v) for v in line], [y1(v) for v in line]
        far_corner = [y1(over_x[0]), x1(over_y[1])]
        mine = line + over_x + over_y + far_corner
        rows_in = mine + [core(v) for v in mine]

        def layout(refs, m):
            pair, i = m // 2, m % 2
            found = []
            for n in range(4):
                base = (n & 1) * 8 + (n >> 1) * 4
                found.append((n, refs[base + pair][i].astype(F32)))
            return found

    else:
        rows_in = lax.all_gather(row, "seq", axis=0, tiled=True)
        rows_in = [lax.all_gather(rows_in, "tensor", axis=2, tiled=True)]

        def layout(refs, m):
            return [(None, refs[0][m].astype(F32))]

    active = pl.pallas_call(
        functools.partial(expert_kernel, layout=layout),
        grid=(experts,),
        out_shape=shape((experts, slots, hidden), BF16),
        in_specs=[
            smem(),
            vmem(),
            vmem(),
            pl.BlockSpec((1, slots, 128), lambda e: (e, 0, 0)),
            pl.BlockSpec((1, model, hidden), lambda e: (e, 0, 0)),
            pl.BlockSpec((1, model, hidden), lambda e: (e, 0, 0)),
        ]
        + [vmem()] * len(rows_in),
        out_specs=pl.BlockSpec((1, slots, hidden), lambda e: (e, 0, 0)),
        scratch_shapes=[pltpu.VMEM((experts, slots, model), BF16)],
        compiler_params=params(),
        name="gate_up",
    )(t1, norm_gain.reshape(1, model), grouped, slot_weight, gate_proj, up_proj, *rows_in)

    def down(columns):
        steps = columns.shape[0]
        return pl.pallas_call(
            down_kernel,
            grid_spec=pltpu.PrefetchScalarGridSpec(
                num_scalar_prefetch=1,
                grid=(steps,),
                in_specs=[
                    vmem(),
                    vmem(),
                    pl.BlockSpec((experts, hidden, width), lambda i, c: (0, 0, c[i])),
                ],
                out_specs=pl.BlockSpec((1, seq, draft, width), lambda i, c: (i, 0, 0, 0)),
                scratch_shapes=[pltpu.VMEM((experts, slots, width), BF16)],
            ),
            out_shape=shape((steps, seq, draft, width), BF16),
            compiler_params=params(),
            name="down",
        )(columns.astype(I32), active, combine, down_proj)

    if not staged:
        sums = down(jnp.arange(tensor, dtype=I32))
        sums = lax.psum_scatter(sums, "tensor", scatter_dimension=0, tiled=True)[0]
        moe = lax.psum_scatter(sums, "seq", scatter_dimension=0, tiled=True)[0]
        mixed_out = (mixed + moe.astype(F32)).astype(BF16)
        return mixed_out, log_sum_exp, key_cache_out, value_cache_out

    other = core(down(jnp.stack([t ^ 1, t ^ 3])))
    own = down(jnp.stack([t, t ^ 2]))

    def split_first(ins, outs):
        a, b = ins
        first_y, first_x, keep_y, keep_x = outs
        for x in range(2):
            for z in range(2):
                first_y[2 * x + z] = (a[1, 4 * x + z].astype(F32) + b[1, 4 * x + z].astype(F32)).astype(BF16)
                keep_y[2 * x + z] = (a[0, 4 * x + z].astype(F32) + b[0, 4 * x + z].astype(F32)).astype(BF16)
        for y in range(2):
            for z in range(2):
                first_x[2 * y + z] = (a[y, 6 + z].astype(F32) + b[y, 6 + z].astype(F32)).astype(BF16)
                keep_x[2 * y + z] = (a[y, 2 + z].astype(F32) + b[y, 2 + z].astype(F32)).astype(BF16)

    four, two, one = shape((4, draft, width), BF16), shape((2, draft, width), BF16), shape((draft, width), BF16)
    first_y, first_x, keep_y, keep_x = small(split_first, (own, other), [four] * 4)
    got_y, got_x = y1(first_y), x1(first_x)

    def split_second(ins, outs):
        keep_a, got_a, keep_b, got_b = ins
        send_a, stay_a, send_b, stay_b = outs
        for keep, got, send, stay in ((keep_a, got_a, send_a, stay_a), (keep_b, got_b, send_b, stay_b)):
            stay[...] = (keep[0:2].astype(F32) + got[0:2].astype(F32)).astype(BF16)
            send[...] = (keep[2:4].astype(F32) + got[2:4].astype(F32)).astype(BF16)

    send_a, stay_a, send_b, stay_b = small(split_second, (keep_y, got_y, keep_x, got_x), [two] * 4)
    got_a, got_b = x1(send_a), y1(send_b)

    def split_third(ins, outs):
        stay, got = (ins[0], ins[2]), (ins[1], ins[3])
        for z in range(4):
            total = stay[z // 2][z % 2].astype(F32) + got[z // 2][z % 2].astype(F32)
            outs[z][...] = total.astype(BF16)

    line = small(split_third, (stay_a, got_a, stay_b, got_b), [one] * 4)
    moe = line[0].astype(F32)
    for z, v in zip(zs, line[1:]):
        moe = moe + z(v).astype(F32)
    mixed_out = (mixed + moe).astype(BF16)
    return mixed_out, log_sum_exp, key_cache_out, value_cache_out


def solution(mesh):
    return jax.shard_map(
        on_device,
        mesh=mesh,
        in_specs=(
            P("seq", "tensor"),
            P("seq", "tensor"),
            P("seq", "tensor"),
            P("seq", None, "tensor"),
            P("seq", None, "tensor"),
            P("seq"),
            P("seq"),
            P(),
            P("seq", None, None),
            P("seq", None),
            P("seq", None),
            P("tensor", None),
            P(),
            P("seq", None, "tensor"),
            P("seq", None, "tensor"),
            P("seq", "tensor", None),
            P("seq", None),
            P("seq", None),
        ),
        out_specs=(
            P("seq", "tensor"),
            P("seq", "tensor"),
            P("seq", None, "tensor"),
            P("seq", None, "tensor"),
        ),
        check_vma=False,
    )
```

```python
import functools
import math

import jax
import jax.numpy as jnp
from jax import lax
from jax.experimental import pallas as pl
from jax.experimental.pallas import tpu as pltpu
from jax.sharding import PartitionSpec as P

HD = 128
CAP = 16
MASKED = -1e30
F32 = jnp.float32
BF16 = jnp.bfloat16
I32 = jnp.int32
STAT = 128
INFO = 16
EXTRA = 256
MIB = 1024 * 1024


def vmem():
    return pl.BlockSpec(memory_space=pltpu.VMEM)


def hbm():
    return pl.BlockSpec(memory_space=pltpu.HBM)


def smem():
    return pl.BlockSpec(memory_space=pltpu.SMEM)


def shape(dims, dtype):
    return jax.ShapeDtypeStruct(dims, dtype)


def in_hbm(v):
    return pltpu.with_memory_space_constraint(v, pltpu.HBM)


def call(kernel, name, ins, in_specs, out_shape, out_specs, scratch=(), limit=16, busy=3):
    ins = [
        in_hbm(v) if spec.memory_space is pltpu.HBM else v
        for v, spec in zip(ins, in_specs)
    ]
    return pl.pallas_call(
        kernel,
        out_shape=out_shape,
        in_specs=in_specs,
        out_specs=out_specs,
        scratch_shapes=list(scratch),
        compiler_params=pltpu.CompilerParams(vmem_limit_bytes=limit * MIB),
        cost_estimate=pl.CostEstimate(flops=0, bytes_accessed=busy * 3_000_000, transcendentals=0),
        name=name,
    )(*ins)


def each(count, body):
    if count <= 16:
        for i in range(count):
            body(i)
    else:

        @pl.loop(0, count)
        def _(i):
            body(i)


def dot(a, b):
    return jnp.dot(a, b, preferred_element_type=F32)


def dot_t(a, b):
    return lax.dot_general(a, b, (((1,), (1,)), ((), ())), preferred_element_type=F32)


def aligned(index, size):
    return index * size if isinstance(index, int) else pl.multiple_of(index * size, size)


def three_parts(value):
    high = value.astype(BF16).astype(F32)
    rest = value - high
    middle = rest.astype(BF16).astype(F32)
    return high, middle, rest - middle


def near_kernel(
    q_hbm, k_hbm, v_hbm, mask_hbm, key_hbm, value_hbm, acc_ref, ids_ref, rw_ref, *refs
):
    out_ref, lse_ref, info_ref, key_ref, value_ref, q_ref, k_ref, v_ref, mask_ref, s_s, w_s, sems = refs
    loads = [
        pltpu.make_async_copy(source, target, sems.at[i])
        for i, (source, target) in enumerate(
            (
                (q_hbm, q_ref),
                (k_hbm, k_ref),
                (v_hbm, v_ref),
                (mask_hbm, mask_ref),
                (key_hbm, key_ref),
                (value_hbm, value_ref),
            )
        )
    ]
    for load in loads:
        load.start()
    for load in loads[:4]:
        load.wait()
    draft, width = q_ref.shape
    scaling = 1.0 / math.sqrt(HD)
    seen = mask_ref[0] > 0
    heads = [slice(h * HD, (h + 1) * HD) for h in range(width // HD)]
    for h, cols in enumerate(heads):
        s_s[h] = jnp.where(seen, dot_t(q_ref[:, cols], k_ref[:, cols]) * scaling, MASKED)
    for h, cols in enumerate(heads):
        lse_ref[:, cols] = jnp.broadcast_to(jnp.max(s_s[h], axis=1, keepdims=True), (draft, HD))
    for h, cols in enumerate(heads):
        top = lse_ref[:, cols]
        weights = jnp.exp(s_s[h] - top[:, 0:draft])
        total = jnp.sum(weights, axis=1, keepdims=True)
        w_s[h] = (weights / total).astype(BF16)
        lse_ref[:, cols] = top + jnp.log(jnp.broadcast_to(total, (draft, HD)))
    for h, cols in enumerate(heads):
        out_ref[:, cols] = dot(w_s[h], v_ref[:, cols])
    accepted = acc_ref.shape[0]
    pick = (lax.broadcasted_iota(I32, (accepted, draft), 1) == acc_ref[...]).astype(F32).astype(BF16)
    rows = jnp.concatenate([dot(pick, k_ref[...]), dot(pick, v_ref[...])], axis=0)
    picks = ids_ref.shape[1]
    info = jnp.zeros((draft, STAT), F32)
    for g, part in enumerate((ids_ref[...].astype(F32), *three_parts(rw_ref[...]))):
        lane = lax.broadcasted_iota(I32, (picks, STAT), 1) - INFO - g * picks
        spread = jnp.where(lane == lax.broadcasted_iota(I32, (picks, STAT), 0), 1.0, 0.0)
        info = info + dot(part.astype(BF16), spread.astype(BF16))
    info_ref[:, 0:STAT] = info
    for g in range(width // 128):
        part = rows[:, g * 128 : (g + 1) * 128]
        info_ref[g * 2 * accepted : (g + 1) * 2 * accepted, STAT:] = part
    for load in loads[4:]:
        load.wait()


def far_kernel(pos_ref, live_ref, key_ref, value_ref, info_ref, *refs, counts, n_out):
    pieces, outs = refs[: len(counts)], refs[len(counts) : len(counts) + n_out]
    q_s, s_s, mp_s, lp_s, op_s, m_s, l_s, o_s = refs[len(counts) + n_out :]
    pages, page_len, width = key_ref.shape
    draft = q_s.shape[1]
    heads = width // HD
    scaling = 1.0 / math.sqrt(HD)
    at = 0
    for piece, count in zip(pieces, counts):
        q_s[at : at + count] = piece[...]
        at += count
    cell = lax.broadcasted_iota(I32, (draft, page_len), 1)
    pairs = [(p, slice(h * HD, (h + 1) * HD)) for p in range(pages) for h in range(heads)]
    for p, cols in pairs:
        scores = dot_t(q_s[pos_ref[p], :, cols], key_ref[p, :, cols]) * scaling
        s_s[p, :, cols] = jnp.where(cell < live_ref[p], scores, MASKED)
    for p, cols in pairs:
        mp_s[p, :, cols] = jnp.broadcast_to(jnp.max(s_s[p, :, cols], axis=1, keepdims=True), (draft, HD))
    for p, cols in pairs:
        weights = jnp.exp(s_s[p, :, cols] - mp_s[p, :, cols])
        lp_s[p, :, cols] = jnp.broadcast_to(jnp.sum(weights, axis=1, keepdims=True), (draft, HD))
        op_s[p, :, cols] = dot(weights.astype(BF16), value_ref[p, :, cols])

    def clear(i):
        m_s[i] = jnp.full((draft, width), MASKED, F32)
        l_s[i] = jnp.zeros((draft, width), F32)
        o_s[i] = jnp.zeros((draft, width), F32)

    each(at, clear)
    for p in range(pages):
        pos = pos_ref[p]
        m_s[pos] = jnp.maximum(m_s[pos], mp_s[p])
    for p in range(pages):
        pos = pos_ref[p]
        scale = jnp.exp(mp_s[p] - m_s[pos])
        l_s[pos] = l_s[pos] + lp_s[p] * scale
        o_s[pos] = o_s[pos] + op_s[p] * scale
    lane = lax.broadcasted_iota(I32, (draft, STAT), 1)

    def finish(i):
        target, row = (outs[i], 0) if n_out > 1 else (outs[0], i)
        stat = jnp.zeros((draft, STAT), F32)
        for h in range(heads):
            cols = slice(h * HD, (h + 1) * HD)
            total = l_s[i, :, cols]
            some = total > 0.0
            safe = jnp.where(some, total, 1.0)
            target[row, :, cols] = (o_s[i, :, cols] / safe).astype(BF16)
            lse = jnp.where(some, m_s[i, :, cols] + jnp.log(safe), MASKED)
            stat = jnp.where(lane % heads == h, lse, stat)
        high, middle, low = three_parts(stat)
        packed = jnp.where(lane < heads, high, jnp.where(lane < 2 * heads, middle, low))
        packed = jnp.where(lane < 3 * heads, packed, info_ref[:, 0:STAT])
        target[row, :, width : width + STAT] = packed.astype(BF16)
        target[row, :, width + STAT :] = info_ref[:, STAT:].astype(BF16)

    each(at, finish)


def merge_kernel(t_ref, near_ref, lse_ref, hidden_ref, w_ref, *refs, counts, n_out):
    pieces, refs = refs[: len(counts)], refs[len(counts) :]
    lse_out, outs = refs[0], refs[1:]
    draft, width = near_ref.shape
    heads = width // HD
    rows = [(piece, i) for piece, count in zip(pieces, counts) for i in range(count)]
    stats = []
    for piece, i in rows:
        packed = piece[i, :, width : width + STAT].astype(F32)
        stats.append(packed + pltpu.roll(packed, STAT - heads, 1) + pltpu.roll(packed, STAT - 2 * heads, 1))
    attended = []
    for h in range(heads):
        cols = slice(h * HD, (h + 1) * HD)
        sums = [s[:, h : h + 1] for s in stats]
        own = lse_ref[:, h * HD : h * HD + 1]
        top = functools.reduce(jnp.maximum, sums, own)
        weight = jnp.exp(own - top)
        total = weight
        summed = near_ref[:, cols] * weight
        for (piece, i), s in zip(rows, sums):
            weight = jnp.exp(s - top)
            total = total + weight
            summed = summed + piece[i, :, cols].astype(F32) * weight
        attended.append((summed / total).astype(BF16))
        lse_out[:, h : h + 1] = top + jnp.log(total)
    attended = jnp.concatenate(attended, axis=1)
    if n_out == 1:
        outs[0][...] = dot(attended, w_ref[...]).astype(outs[0].dtype)
        return
    for n in range(n_out):
        start = pl.multiple_of((t_ref[0] ^ n) * width, width)
        part = dot(attended, w_ref[:, pl.ds(start, width)])
        if n == 0:
            part = part + hidden_ref[:, pl.ds(start, width)].astype(F32)
        outs[n][...] = part.astype(outs[n].dtype)


def slots_kernel(me_ref, after_hbm, *refs, counts, picks, at_column):
    pieces, (g_ref, c_ref, w_ref) = refs[: len(counts)], refs[len(counts) :]
    draft = g_ref.shape[2]
    experts = w_ref.shape[0]
    row, column = (lax.broadcasted_iota(I32, (draft, draft), axis) for axis in (0, 1))
    upper = jnp.where(row < column, 1.0, 0.0).astype(BF16)
    same = jnp.where(row == column, 1.0, 0.0).astype(BF16)
    number = lax.broadcasted_iota(I32, (CAP, draft), 0).astype(F32)
    first = me_ref[0] * experts

    def one(piece, i, m):
        info = jnp.transpose(piece[i, :, at_column : at_column + STAT].astype(F32))
        ids, *parts = (info[INFO + g * picks : INFO + (g + 1) * picks] for g in range(4))
        weight = parts[0] + parts[1] + parts[2]
        hits, weights = [], []
        for e in range(experts):
            hit = ids == (first + e).astype(F32)
            hits.append(jnp.max(jnp.where(hit, 1.0, 0.0), axis=0, keepdims=True))
            weights.append(jnp.sum(jnp.where(hit, weight, 0.0), axis=0, keepdims=True))
        table = jnp.concatenate(hits + [jnp.zeros((16 - experts, draft), F32)], axis=0)
        rank = dot(table.astype(BF16), upper)
        blocks = []
        for e in range(experts):
            block = jnp.where((number == rank[e : e + 1]) & (hits[e] > 0.0), 1.0, 0.0)
            blocks.append(block)
            row_weight = jnp.sum(block * weights[e], axis=1, keepdims=True)
            w_ref[e, pl.ds(aligned(m, CAP), CAP), :] = jnp.broadcast_to(row_weight, (CAP, 128))
        stacked = jnp.concatenate(blocks, axis=0).astype(BF16)
        g_ref[m] = stacked
        c_ref[m] = dot_t(same, stacked).astype(BF16)

    at = 0
    for piece, count in zip(pieces, counts):
        each(count, lambda i, piece=piece, at=at: one(piece, i, at + i))
        at += count


def mix_kernel(own_ref, a_ref, b_ref, c_ref, after_hbm, mixed_ref, row_ref):
    mixed = own_ref[...] + a_ref[...].astype(F32) + b_ref[...].astype(F32) + c_ref[...].astype(F32)
    mixed_ref[...] = mixed
    row_ref[0] = mixed.astype(BF16)


def cache_kernel(pos_ref, live_ref, key_ref, value_ref, after_hbm, *refs, counts, accept):
    pieces, (key_out, value_out, mark_ref, table) = refs[: len(counts)], refs[len(counts) :]
    block, page_len, width = key_ref.shape
    step = pl.program_id(0)

    @pl.when(step == 0)
    def _():
        at = 0
        for piece, count in zip(pieces, counts):
            for g in range(width // 128):
                rows = slice(g * 2 * accept, (g + 1) * 2 * accept)
                table[at : at + count, :, g * 128 : (g + 1) * 128] = piece[:, rows, width + STAT :]
            at += count
        mark_ref[...] = jnp.zeros_like(mark_ref)

    key_out[...] = key_ref[...]
    value_out[...] = value_ref[...]
    for i in range(block):
        p = step * block + i
        live = live_ref[p]

        @pl.when((live > -accept) & (live < page_len))
        def _():
            rows = table[pos_ref[p]]
            offset = lax.broadcasted_iota(I32, (page_len, 2 * accept), 0) - live
            column = lax.broadcasted_iota(I32, (page_len, 2 * accept), 1)
            cell = lax.broadcasted_iota(I32, (page_len, width), 0) - live
            touched = (cell >= 0) & (cell < accept)
            for source, out, shift in ((key_ref, key_out, 0), (value_ref, value_out, accept)):
                hit = (offset == column - shift) & (offset >= 0) & (offset < accept)
                place = jnp.where(hit, 1.0, 0.0).astype(BF16)
                out[i] = jnp.where(touched, dot(place, rows), source[i].astype(F32)).astype(BF16)


def combine_rows(active_ref, down_ref, c_ref, y_s, put):
    experts = active_ref.shape[0]
    groups = c_ref.shape[0]
    for e in range(experts):
        y = dot(active_ref[e], down_ref[e]).astype(BF16)
        for m in range(groups):
            y_s[m, e * CAP : (e + 1) * CAP, :] = y[m * CAP : (m + 1) * CAP]
    each(groups, lambda m: put(m, dot(c_ref[m], y_s[m])))


def down_loads(cols_ref, first, down_hbm, down_s, sems):
    width = down_s.shape[3]
    loads = []
    for i in range(down_s.shape[0]):
        cols = pl.ds(pl.multiple_of(cols_ref[first + i] * width, width), width)
        loads.append(pltpu.make_async_copy(down_hbm.at[:, :, cols], down_s.at[i], sems.at[i]))
    return loads


def expert_kernel(
    t_ref, cols_ref, gain_ref, g_ref, rw_ref, c_ref, gate_hbm, up_hbm, down_hbm, *refs, layout, put, steps
):
    later = len(steps) - 1
    pieces, refs = refs[: -10 - 2 * len(steps)], refs[-10 - 2 * len(steps) :]
    active_ref, out_ref, refs = refs[0], refs[1], refs[2:]
    later, (xs, xn, sc, down_s, y_s, gate_s, up_s, gate_sem, up_sem, *sems) = refs[:later], refs[later:]
    experts, slots, model = xs.shape
    groups = g_ref.shape[0]
    weights = [
        (
            pltpu.make_async_copy(gate_hbm.at[e], gate_s.at[e], gate_sem.at[e]),
            pltpu.make_async_copy(up_hbm.at[e], up_s.at[e], up_sem.at[e]),
        )
        for e in range(experts)
    ]
    buffers = [down_s, *later]
    loads = [down_loads(cols_ref, first, down_hbm, to, sem) for first, to, sem in zip(steps, buffers, sems)]
    queue = weights + [(load,) for some in loads for load in some]
    ahead = 3
    for some in queue[:ahead]:
        for load in some:
            load.start()

    def columns(n, width):
        return slice(0, width) if n is None else pl.ds(pl.multiple_of((t_ref[0] ^ n) * width, width), width)

    def squares(m, j):
        total = sum(jnp.sum(v * v, axis=1, keepdims=True) for _, v in layout(pieces, m))
        sc[j] = jnp.broadcast_to(lax.rsqrt(total / model + 1e-6), sc.shape[1:])

    def scaled(m, j):
        for n, v in layout(pieces, m):
            cols = columns(n, v.shape[1])
            xn[j, :, cols] = (v * sc[j, :, 0:1] * gain_ref[:, cols]).astype(BF16)

    def picked(m, j):
        rows = dot(g_ref[m], xn[j]).astype(BF16)
        for i in range(experts):
            xs[i, pl.ds(aligned(m, CAP), CAP), :] = rows[i * CAP : (i + 1) * CAP]

    lap = xn.shape[0]

    def requests(i):
        for step in (squares, scaled, picked):
            for j in range(lap):
                step(i * lap + j, j)

    each(groups // lap, requests)
    def arrived(i):
        for load in queue[i]:
            load.wait()
        for load in queue[i + ahead] if i + ahead < len(queue) else ():
            load.start()

    for e in range(experts):
        arrived(e)
        gate = dot(xs[e], gate_s[e])
        up = dot(xs[e], up_s[e])
        active = gate / (1.0 + jnp.exp(-gate)) * up
        active_ref[e] = (active * rw_ref[e, :, 0:1]).astype(BF16)
    for i in range(len(loads[0])):
        arrived(experts + i)
        combine_rows(active_ref, down_s.at[i], c_ref, y_s, functools.partial(put, out_ref, i))
    for i in range(experts + len(loads[0]), len(queue)):
        arrived(i)


def down_kernel(active_ref, c_ref, add_ref, down_ref, *refs, put):
    outs, y_s = refs[:-1], refs[-1]
    for i in range(down_ref.shape[0]):
        combine_rows(active_ref, down_ref.at[i], c_ref, y_s, functools.partial(put, outs, add_ref, i))


def put_plain(out_ref, i, m, value):
    out_ref[i, m] = value.astype(BF16)


def put_added(outs, add_ref, i, m, value):
    value = (value + add_ref[i, m].astype(F32)).astype(BF16)
    side, z = 2 * i + m // 4, m % 4
    if z == 0:
        outs[side][...] = value
    else:
        outs[4 + side][z - 1] = value


def total_kernel(own_ref, x_ref, y_ref, d_ref, mark_ref, *outs):
    for z in range(3):
        total = own_ref[z].astype(F32) + x_ref[z].astype(F32) + y_ref[z].astype(F32) + d_ref[z].astype(F32)
        outs[z][...] = total.astype(BF16)


def on_device(
    queries,
    draft_keys,
    draft_values,
    key_cache,
    value_cache,
    page_request,
    page_slot,
    cache_len,
    tree_mask,
    accepted,
    hidden_in,
    out_proj,
    norm_gain,
    gate_proj,
    up_proj,
    down_proj,
    expert_ids,
    route_weight,
):
    draft, width = queries.shape
    pages, page_len, _ = key_cache.shape
    model = hidden_in.shape[1]
    heads = width // HD
    seq, tensor = lax.axis_size("seq"), lax.axis_size("tensor")
    experts = gate_proj.shape[0]
    hidden = gate_proj.shape[2]
    accept = accepted.shape[1]
    slots = seq * CAP
    staged = seq == 8 and tensor == 4
    me, t = lax.axis_index("seq"), lax.axis_index("tensor")

    def hop(axis, mask):
        size = seq if axis == "seq" else tensor
        pairs = [(i, i ^ mask) for i in range(size)]
        return lambda v: lax.ppermute(v, axis, pairs)

    x1, y1, core = hop("seq", 1), hop("tensor", 2), hop("tensor", 1)
    zs = [hop("seq", 2 * k) for k in (1, 2, 3)]
    big = 16 if staged else 56

    def diagonal(v):
        flip = tensor + 2
        return lax.ppermute(v, ("seq", "tensor"), [(i, i ^ flip) for i in range(seq * tensor)])

    relative = page_request ^ me if staged else page_request
    pos = (relative & 1) * 4 + (relative >> 1) if staged else relative
    pos = pos.astype(I32)
    request_hit = page_request[:, None] == jnp.arange(cache_len.shape[0], dtype=I32)[None, :]
    live = jnp.sum(jnp.where(request_hit, cache_len[None, :], 0), axis=1) - page_slot * page_len
    me1, t1 = me.reshape(1).astype(I32), t.reshape(1).astype(I32)

    if staged:
        own = queries[None]
        beside = x1(own)
        line = [z(own) for z in zs]
        every_query = [own, *line, beside, *[x1(b) for b in line]]
    else:
        every_query = [lax.all_gather(queries[None], "seq", axis=0, tiled=True)]
    counts = tuple(a.shape[0] for a in every_query)

    near_out, near_lse, info, keys, values = call(
        near_kernel,
        "near",
        (
            queries,
            draft_keys,
            draft_values,
            tree_mask,
            key_cache,
            value_cache,
            accepted.reshape(accept, 1),
            expert_ids,
            route_weight,
        ),
        [hbm()] * 6 + [vmem()] * 3,
        [
            shape((draft, width), F32),
            shape((draft, width), F32),
            shape((draft, EXTRA), F32),
            shape(key_cache.shape, BF16),
            shape(value_cache.shape, BF16),
        ],
        [vmem()] * 5,
        [
            *[pltpu.VMEM((draft, width), BF16)] * 3,
            pltpu.VMEM((1, draft, draft), I32),
            pltpu.VMEM((heads, draft, draft), F32),
            pltpu.VMEM((heads, draft, draft), BF16),
            pltpu.SemaphoreType.DMA((6,)),
        ],
        busy=2,
    )

    n_out = seq if staged else 1
    state = pltpu.VMEM((seq, draft, width), F32)
    per_page = pltpu.VMEM((pages, draft, width), F32)
    partials = call(
        functools.partial(far_kernel, counts=counts, n_out=n_out),
        "far",
        (pos, live, keys, values, info, *every_query),
        [smem(), smem()] + [vmem()] * (3 + len(every_query)),
        [shape((seq // n_out, draft, width + EXTRA), BF16)] * n_out,
        [vmem()] * n_out,
        [pltpu.VMEM((seq, draft, width), BF16), *[per_page] * 4, *[state] * 3],
        limit=big,
        busy=5,
    )

    if staged:
        back = [partials[0]]
        for place in range(1, 8):
            back.append(hop("seq", (place & 3) * 2 + (place >> 2))(partials[place]))
    else:
        back = [lax.all_to_all(partials[0], "seq", split_axis=0, concat_axis=0, tiled=True)]

    n_parts = tensor if staged else 1
    part_shape = (
        [shape((draft, width), F32)] + [shape((draft, width), BF16)] * 3 if staged else [shape((draft, model), F32)]
    )
    back_counts = tuple(b.shape[0] for b in back)
    log_sum_exp, *parts = call(
        functools.partial(merge_kernel, counts=back_counts, n_out=n_parts),
        "merge",
        (t1, near_out, near_lse, hidden_in, out_proj, *back),
        [smem()] + [vmem()] * (4 + len(back)),
        [shape((draft, heads), F32)] + part_shape,
        [vmem()] * (1 + n_parts),
        limit=big,
        busy=4,
    )

    grouped, combine, slot_weight = call(
        functools.partial(slots_kernel, counts=back_counts, picks=expert_ids.shape[1], at_column=width),
        "slots",
        (me1, parts[0], *back),
        [smem(), hbm()] + [vmem()] * len(back),
        [
            shape((seq, experts * CAP, draft), BF16),
            shape((seq, draft, experts * CAP), BF16),
            shape((experts, slots, 128), F32),
        ],
        [vmem()] * 3,
        limit=big,
    )

    if staged:
        got = [hop("tensor", n)(parts[n]) for n in (1, 2, 3)]
        mixed, row = call(
            mix_kernel,
            "mix",
            (parts[0], *got, slot_weight),
            [vmem()] * 4 + [hbm()],
            [shape((draft, width), F32), shape((1, draft, width), BF16)],
            [vmem()] * 2,
            busy=1,
        )
    else:
        summed = lax.psum(parts[0], "tensor") + hidden_in.astype(F32)
        mixed = lax.dynamic_slice_in_dim(summed, t * width, width, 1)
        row = mixed.astype(BF16)[None]

    if staged:
        line = [z(row) for z in zs]
        near_by = [row, x1(row), y1(row), diagonal(row)]
        line = jnp.concatenate(line)
        far_off = [line, x1(line), y1(line), diagonal(line)]
        rows_in = near_by + far_off + [core(jnp.concatenate(near_by))] + [core(v) for v in far_off]

        def layout(refs, m):
            found = []
            for n in range(4):
                side, z = (n >> 1) * 2 + m // 4, m % 4
                if n & 1:
                    v = refs[8][side] if z == 0 else refs[9 + side][z - 1]
                else:
                    v = refs[side][0] if z == 0 else refs[4 + side][z - 1]
                found.append((n, v.astype(F32)))
            return found

        columns, steps, n_down = jnp.stack([t ^ 1, t ^ 3, t, t ^ 2]).astype(I32), (0, 2), 2
    else:
        rows_in = lax.all_gather(row, "seq", axis=0, tiled=True)
        rows_in = [lax.all_gather(rows_in, "tensor", axis=2, tiled=True)]

        def layout(refs, m):
            return [(None, refs[0][m].astype(F32))]

        columns, steps, n_down = jnp.arange(tensor, dtype=I32), (0,), tensor

    y_scratch = pltpu.VMEM((seq, experts * CAP, width), BF16)
    down_block = (n_down, experts, hidden, width)
    later = [shape(down_block, BF16)] * (len(steps) - 1)
    lap = math.gcd(seq, 8)
    active, sums, *later = call(
        functools.partial(expert_kernel, layout=layout, put=put_plain, steps=steps),
        "experts",
        (
            t1,
            columns,
            norm_gain.reshape(1, model),
            grouped,
            slot_weight,
            combine,
            gate_proj,
            up_proj,
            down_proj,
            *rows_in,
        ),
        [smem()] * 2 + [vmem()] * 4 + [hbm()] * 3 + [vmem()] * len(rows_in),
        [
            shape((experts, slots, hidden), BF16),
            shape((n_down, seq, draft, width), BF16),
            *later,
        ],
        [vmem()] * (2 + len(later)),
        [
            pltpu.VMEM((experts, slots, model), BF16),
            pltpu.VMEM((lap, draft, model), BF16),
            pltpu.VMEM((lap, draft, 128), F32),
            pltpu.VMEM(down_block, BF16),
            y_scratch,
            *[pltpu.VMEM((experts, model, hidden), BF16)] * 2,
            *[pltpu.SemaphoreType.DMA((experts,))] * 2,
            *[pltpu.SemaphoreType.DMA((n_down,))] * len(steps),
        ],
        limit=36 if staged else 60,
        busy=9,
    )

    if staged:
        sums = call(
            functools.partial(down_kernel, put=put_added),
            "down",
            (active, combine, core(sums), *later),
            [vmem()] * 4,
            [shape((draft, width), BF16)] * 4 + [shape((3, draft, width), BF16)] * 4,
            [vmem()] * 8,
            [y_scratch],
            busy=3,
        )
        first_sums = sums[0]
    else:
        first_sums = sums
    block = 4 if pages % 4 == 0 else 1
    page_spec = pl.BlockSpec((block, page_len, width), lambda p: (p, 0, 0))
    key_cache_out, value_cache_out, cache_mark = pl.pallas_call(
        functools.partial(cache_kernel, counts=back_counts, accept=accept),
        grid=(pages // block,),
        out_shape=[shape(key_cache.shape, BF16), shape(value_cache.shape, BF16), shape((8, 128), F32)],
        in_specs=[smem(), smem(), page_spec, page_spec, hbm()] + [vmem()] * len(back),
        out_specs=[page_spec, page_spec, pl.BlockSpec((8, 128), lambda p: (0, 0))],
        scratch_shapes=[pltpu.VMEM((seq, 2 * accept, width), BF16)],
        compiler_params=pltpu.CompilerParams(vmem_limit_bytes=big * MIB),
        cost_estimate=pl.CostEstimate(flops=0, bytes_accessed=12_000_000, transcendentals=0),
        name="cache",
    )(pos, live, in_hbm(key_cache), in_hbm(value_cache), in_hbm(first_sums), *back)

    if not staged:
        sums = lax.psum_scatter(sums, "tensor", scatter_dimension=0, tiled=True)[0]
        moe = lax.psum_scatter(sums, "seq", scatter_dimension=0, tiled=True)[0]
        mixed_out = (mixed + moe.astype(F32)).astype(BF16)
        return mixed_out, log_sum_exp, key_cache_out, value_cache_out

    line = call(
        total_kernel,
        "total",
        (sums[4], x1(sums[5]), y1(sums[6]), diagonal(sums[7]), cache_mark),
        [vmem()] * 5,
        [shape((draft, width), BF16)] * 3,
        [vmem()] * 3,
        busy=1,
    )
    moe = sums[0].astype(F32)
    for z, v in zip(zs, line):
        moe = moe + z(v).astype(F32)
    for move, v in zip((x1, y1, diagonal), sums[1:4]):
        moe = moe + move(v).astype(F32)
    mixed_out = (mixed + moe).astype(BF16)
    return mixed_out, log_sum_exp, key_cache_out, value_cache_out


def solution(mesh):
    return jax.shard_map(
        on_device,
        mesh=mesh,
        in_specs=(
            P("seq", "tensor"),
            P("seq", "tensor"),
            P("seq", "tensor"),
            P("seq", None, "tensor"),
            P("seq", None, "tensor"),
            P("seq"),
            P("seq"),
            P(),
            P("seq", None, None),
            P("seq", None),
            P("seq", None),
            P("tensor", None),
            P(),
            P("seq", None, "tensor"),
            P("seq", None, "tensor"),
            P("seq", "tensor", None),
            P("seq", None),
            P("seq", None),
        ),
        out_specs=(
            P("seq", "tensor"),
            P("seq", "tensor"),
            P("seq", None, "tensor"),
            P("seq", None, "tensor"),
        ),
        check_vma=False,
    )
```

```python
import functools
import math

import jax
import jax.numpy as jnp
from jax import lax
from jax.experimental import pallas as pl
from jax.experimental.pallas import tpu as pltpu
from jax.sharding import PartitionSpec as P

HD = 128
CAP = 16
MASKED = -1e30
F32 = jnp.float32
BF16 = jnp.bfloat16
I32 = jnp.int32
STAT = 128
INFO = 16
EXTRA = 256
MIB = 1024 * 1024


def vmem():
    return pl.BlockSpec(memory_space=pltpu.VMEM)


def hbm():
    return pl.BlockSpec(memory_space=pltpu.HBM)


def smem():
    return pl.BlockSpec(memory_space=pltpu.SMEM)


def shape(dims, dtype):
    return jax.ShapeDtypeStruct(dims, dtype)


def in_hbm(v):
    return pltpu.with_memory_space_constraint(v, pltpu.HBM)


def call(kernel, name, ins, in_specs, out_shape, out_specs, scratch=(), limit=16, busy=3):
    ins = [
        in_hbm(v) if spec.memory_space is pltpu.HBM else v
        for v, spec in zip(ins, in_specs)
    ]
    return pl.pallas_call(
        kernel,
        out_shape=out_shape,
        in_specs=in_specs,
        out_specs=out_specs,
        scratch_shapes=list(scratch),
        compiler_params=pltpu.CompilerParams(vmem_limit_bytes=limit * MIB),
        cost_estimate=pl.CostEstimate(flops=0, bytes_accessed=busy * 3_000_000, transcendentals=0),
        name=name,
    )(*ins)


def each(count, body):
    if count <= 16:
        for i in range(count):
            body(i)
    else:

        @pl.loop(0, count)
        def _(i):
            body(i)


def dot(a, b):
    return jnp.dot(a, b, preferred_element_type=F32)


def dot_t(a, b):
    return lax.dot_general(a, b, (((1,), (1,)), ((), ())), preferred_element_type=F32)


def dot_0(a, b):
    return lax.dot_general(a, b, (((0,), (0,)), ((), ())), preferred_element_type=F32)


def aligned(index, size):
    return index * size if isinstance(index, int) else pl.multiple_of(index * size, size)


def three_parts(value):
    high = value.astype(BF16).astype(F32)
    rest = value - high
    middle = rest.astype(BF16).astype(F32)
    return high, middle, rest - middle


def near_kernel(
    q_hbm, k_hbm, v_hbm, mask_hbm, key_hbm, value_hbm, acc_ref, ids_ref, rw_ref, *refs
):
    out_ref, lse_ref, info_ref, key_ref, value_ref, q_ref, k_ref, v_ref, mask_ref, s_s, w_s, sems = refs
    loads = [
        pltpu.make_async_copy(source, target, sems.at[i])
        for i, (source, target) in enumerate(
            (
                (q_hbm, q_ref),
                (k_hbm, k_ref),
                (v_hbm, v_ref),
                (mask_hbm, mask_ref),
                (key_hbm, key_ref),
                (value_hbm, value_ref),
            )
        )
    ]
    for load in loads:
        load.start()
    for load in loads[:4]:
        load.wait()
    draft, width = q_ref.shape
    scaling = 1.0 / math.sqrt(HD)
    seen = mask_ref[0] > 0
    heads = [slice(h * HD, (h + 1) * HD) for h in range(width // HD)]
    for h, cols in enumerate(heads):
        s_s[h] = jnp.where(seen, dot_t(q_ref[:, cols], k_ref[:, cols]) * scaling, MASKED)
    for h, cols in enumerate(heads):
        lse_ref[:, cols] = jnp.broadcast_to(jnp.max(s_s[h], axis=1, keepdims=True), (draft, HD))
    for h, cols in enumerate(heads):
        top = lse_ref[:, cols]
        weights = jnp.exp(s_s[h] - top[:, 0:draft])
        total = jnp.sum(weights, axis=1, keepdims=True)
        w_s[h] = (weights / total).astype(BF16)
        lse_ref[:, cols] = top + jnp.log(jnp.broadcast_to(total, (draft, HD)))
    for h, cols in enumerate(heads):
        out_ref[:, cols] = dot(w_s[h], v_ref[:, cols])
    accepted = acc_ref.shape[1]
    pick = (lax.broadcasted_iota(I32, (draft, accepted), 0) == acc_ref[...]).astype(F32).astype(BF16)
    rows = jnp.concatenate([dot_0(pick, k_ref[...]), dot_0(pick, v_ref[...])], axis=0)
    picks = ids_ref.shape[0]
    info = jnp.zeros((draft, STAT), F32)
    for g, part in enumerate((ids_ref[...].astype(F32), *three_parts(rw_ref[...]))):
        lane = lax.broadcasted_iota(I32, (picks, STAT), 1) - INFO - g * picks
        spread = jnp.where(lane == lax.broadcasted_iota(I32, (picks, STAT), 0), 1.0, 0.0)
        info = info + dot_0(part.astype(BF16), spread.astype(BF16))
    info_ref[:, 0:STAT] = info
    for g in range(width // 128):
        part = rows[:, g * 128 : (g + 1) * 128]
        info_ref[g * 2 * accepted : (g + 1) * 2 * accepted, STAT:] = part
    for load in loads[4:]:
        load.wait()


def far_kernel(pos_ref, live_ref, key_ref, value_ref, info_ref, *refs, counts, n_out):
    pieces, outs = refs[: len(counts)], refs[len(counts) : len(counts) + n_out]
    q_s, s_s, mp_s, lp_s, op_s, m_s, l_s, o_s = refs[len(counts) + n_out :]
    pages, page_len, width = key_ref.shape
    draft = q_s.shape[1]
    heads = width // HD
    scaling = 1.0 / math.sqrt(HD)
    at = 0
    for piece, count in zip(pieces, counts):
        q_s[at : at + count] = piece[...]
        at += count
    cell = lax.broadcasted_iota(I32, (draft, page_len), 1)
    pairs = [(p, slice(h * HD, (h + 1) * HD)) for p in range(pages) for h in range(heads)]
    for p, cols in pairs:
        scores = dot_t(q_s[pos_ref[p], :, cols], key_ref[p, :, cols]) * scaling
        s_s[p, :, cols] = jnp.where(cell < live_ref[p], scores, MASKED)
    for p, cols in pairs:
        mp_s[p, :, cols] = jnp.broadcast_to(jnp.max(s_s[p, :, cols], axis=1, keepdims=True), (draft, HD))
    for p, cols in pairs:
        weights = jnp.exp(s_s[p, :, cols] - mp_s[p, :, cols])
        lp_s[p, :, cols] = jnp.broadcast_to(jnp.sum(weights, axis=1, keepdims=True), (draft, HD))
        op_s[p, :, cols] = dot(weights.astype(BF16), value_ref[p, :, cols])

    def clear(i):
        m_s[i] = jnp.full((draft, width), MASKED, F32)
        l_s[i] = jnp.zeros((draft, width), F32)
        o_s[i] = jnp.zeros((draft, width), F32)

    each(at, clear)
    for p in range(pages):
        pos = pos_ref[p]
        m_s[pos] = jnp.maximum(m_s[pos], mp_s[p])
    for p in range(pages):
        pos = pos_ref[p]
        scale = jnp.exp(mp_s[p] - m_s[pos])
        l_s[pos] = l_s[pos] + lp_s[p] * scale
        o_s[pos] = o_s[pos] + op_s[p] * scale
    lane = lax.broadcasted_iota(I32, (draft, STAT), 1)

    def finish(i):
        target, row = (outs[i], 0) if n_out > 1 else (outs[0], i)
        stat = jnp.zeros((draft, STAT), F32)
        for h in range(heads):
            cols = slice(h * HD, (h + 1) * HD)
            total = l_s[i, :, cols]
            some = total > 0.0
            safe = jnp.where(some, total, 1.0)
            target[row, :, cols] = (o_s[i, :, cols] / safe).astype(BF16)
            lse = jnp.where(some, m_s[i, :, cols] + jnp.log(safe), MASKED)
            stat = jnp.where(lane % heads == h, lse, stat)
        high, middle, low = three_parts(stat)
        packed = jnp.where(lane < heads, high, jnp.where(lane < 2 * heads, middle, low))
        packed = jnp.where(lane < 3 * heads, packed, info_ref[:, 0:STAT])
        target[row, :, width : width + STAT] = packed.astype(BF16)
        target[row, :, width + STAT :] = info_ref[:, STAT:].astype(BF16)

    each(at, finish)


def merge_kernel(t_ref, near_ref, lse_ref, hidden_ref, w_ref, *refs, counts, n_out):
    pieces, refs = refs[: len(counts)], refs[len(counts) :]
    lse_out, outs = refs[0], refs[1:]
    draft, width = near_ref.shape
    heads = width // HD
    rows = [(piece, i) for piece, count in zip(pieces, counts) for i in range(count)]
    stats = []
    for piece, i in rows:
        packed = piece[i, :, width : width + STAT].astype(F32)
        stats.append(packed + pltpu.roll(packed, STAT - heads, 1) + pltpu.roll(packed, STAT - 2 * heads, 1))
    attended = []
    for h in range(heads):
        cols = slice(h * HD, (h + 1) * HD)
        sums = [s[:, h : h + 1] for s in stats]
        own = lse_ref[:, h * HD : h * HD + 1]
        top = functools.reduce(jnp.maximum, sums, own)
        weight = jnp.exp(own - top)
        total = weight
        summed = near_ref[:, cols] * weight
        for (piece, i), s in zip(rows, sums):
            weight = jnp.exp(s - top)
            total = total + weight
            summed = summed + piece[i, :, cols].astype(F32) * weight
        attended.append((summed / total).astype(BF16))
        lse_out[:, h : h + 1] = top + jnp.log(total)
    attended = jnp.concatenate(attended, axis=1)
    if n_out == 1:
        outs[0][...] = dot(attended, w_ref[...]).astype(outs[0].dtype)
        return
    for n in range(n_out):
        start = pl.multiple_of((t_ref[0] ^ n) * width, width)
        part = dot(attended, w_ref[:, pl.ds(start, width)])
        if n == 0:
            part = part + hidden_ref[:, pl.ds(start, width)].astype(F32)
        outs[n][...] = part.astype(outs[n].dtype)


def slots_kernel(me_ref, after_ref, *refs, counts, picks, at_column):
    pieces, (g_ref, c_ref, w_ref) = refs[: len(counts)], refs[len(counts) :]
    draft = g_ref.shape[2]
    experts = w_ref.shape[0]
    row, column = (lax.broadcasted_iota(I32, (draft, draft), axis) for axis in (0, 1))
    upper = jnp.where(row < column, 1.0, 0.0).astype(BF16)
    same = jnp.where(row == column, 1.0, 0.0).astype(BF16)
    number = lax.broadcasted_iota(I32, (CAP, draft), 0).astype(F32)
    first = me_ref[0] * experts

    def one(piece, i, m):
        info = jnp.transpose(piece[i, :, at_column : at_column + STAT].astype(F32))
        ids, *parts = (info[INFO + g * picks : INFO + (g + 1) * picks] for g in range(4))
        weight = parts[0] + parts[1] + parts[2]
        hits, weights = [], []
        for e in range(experts):
            hit = ids == (first + e).astype(F32)
            hits.append(jnp.max(jnp.where(hit, 1.0, 0.0), axis=0, keepdims=True))
            weights.append(jnp.sum(jnp.where(hit, weight, 0.0), axis=0, keepdims=True))
        table = jnp.concatenate(hits + [jnp.zeros((16 - experts, draft), F32)], axis=0)
        rank = dot(table.astype(BF16), upper)
        blocks = []
        for e in range(experts):
            block = jnp.where((number == rank[e : e + 1]) & (hits[e] > 0.0), 1.0, 0.0)
            blocks.append(block)
            row_weight = jnp.sum(block * weights[e], axis=1, keepdims=True)
            w_ref[e, pl.ds(aligned(m, CAP), CAP), :] = jnp.broadcast_to(row_weight, (CAP, 128))
        stacked = jnp.concatenate(blocks, axis=0).astype(BF16)
        g_ref[m] = stacked
        c_ref[m] = dot_t(same, stacked).astype(BF16)

    at = 0
    for piece, count in zip(pieces, counts):
        each(count, lambda i, piece=piece, at=at: one(piece, i, at + i))
        at += count


def mix_kernel(own_ref, a_ref, b_ref, c_ref, after_ref, mixed_ref, row_ref):
    mixed = own_ref[...] + a_ref[...].astype(F32) + b_ref[...].astype(F32) + c_ref[...].astype(F32)
    mixed_ref[...] = mixed
    row_ref[0] = mixed.astype(BF16)


def cache_kernel(pos_ref, live_ref, key_ref, value_ref, after_ref, *refs, counts, accept):
    pieces, (key_out, value_out, mark_ref, table) = refs[: len(counts)], refs[len(counts) :]
    block, page_len, width = key_ref.shape
    step = pl.program_id(0)

    @pl.when(step == 0)
    def _():
        at = 0
        for piece, count in zip(pieces, counts):
            for g in range(width // 128):
                rows = slice(g * 2 * accept, (g + 1) * 2 * accept)
                table[at : at + count, :, g * 128 : (g + 1) * 128] = piece[:, rows, width + STAT :]
            at += count
        mark_ref[...] = jnp.zeros_like(mark_ref)

    key_out[...] = key_ref[...]
    value_out[...] = value_ref[...]
    for i in range(block):
        p = step * block + i
        live = live_ref[p]

        @pl.when((live > -accept) & (live < page_len))
        def _():
            rows = table[pos_ref[p]]
            offset = lax.broadcasted_iota(I32, (page_len, 2 * accept), 0) - live
            column = lax.broadcasted_iota(I32, (page_len, 2 * accept), 1)
            cell = lax.broadcasted_iota(I32, (page_len, width), 0) - live
            touched = (cell >= 0) & (cell < accept)
            for source, out, shift in ((key_ref, key_out, 0), (value_ref, value_out, accept)):
                hit = (offset == column - shift) & (offset >= 0) & (offset < accept)
                place = jnp.where(hit, 1.0, 0.0).astype(BF16)
                out[i] = jnp.where(touched, dot(place, rows), source[i].astype(F32)).astype(BF16)


def combine_rows(active_ref, down_ref, c_ref, y_s, put):
    experts = active_ref.shape[0]
    groups = c_ref.shape[0]
    for e in range(experts):
        y = dot(active_ref[e], down_ref[e]).astype(BF16)
        for m in range(groups):
            y_s[m, e * CAP : (e + 1) * CAP, :] = y[m * CAP : (m + 1) * CAP]
    each(groups, lambda m: put(m, dot(c_ref[m], y_s[m])))


def down_loads(cols_ref, first, down_hbm, down_s, sems):
    width = down_s.shape[3]
    loads = []
    for i in range(down_s.shape[0]):
        cols = pl.ds(pl.multiple_of(cols_ref[first + i] * width, width), width)
        loads.append(pltpu.make_async_copy(down_hbm.at[:, :, cols], down_s.at[i], sems.at[i]))
    return loads


def stack_kernel(*refs):
    for i, block in enumerate(refs[:-1]):
        refs[-1][i] = block[0]


def expert_kernel(
    t_ref, cols_ref, gain_ref, g_ref, rw_ref, c_ref, gate_hbm, up_hbm, down_hbm, *refs, layout, put, steps
):
    later = len(steps) - 1
    pieces, refs = refs[: -10 - 2 * len(steps)], refs[-10 - 2 * len(steps) :]
    active_ref, out_ref, refs = refs[0], refs[1], refs[2:]
    later, (xs, xn, sc, down_s, y_s, gate_s, up_s, gate_sem, up_sem, *sems) = refs[:later], refs[later:]
    experts, slots, model = xs.shape
    groups = g_ref.shape[0]
    weights = [
        (
            pltpu.make_async_copy(gate_hbm.at[e], gate_s.at[e], gate_sem.at[e]),
            pltpu.make_async_copy(up_hbm.at[e], up_s.at[e], up_sem.at[e]),
        )
        for e in range(experts)
    ]
    buffers = [down_s, *later]
    loads = [down_loads(cols_ref, first, down_hbm, to, sem) for first, to, sem in zip(steps, buffers, sems)]
    for some in weights:
        for load in some:
            load.start()
    for load in loads[0]:
        load.start()

    def columns(n, width):
        return slice(0, width) if n is None else pl.ds(pl.multiple_of((t_ref[0] ^ n) * width, width), width)

    def squares(m, j):
        total = sum(jnp.sum(v * v, axis=1, keepdims=True) for _, v in layout(pieces, m))
        sc[j] = jnp.broadcast_to(lax.rsqrt(total / model + 1e-6), sc.shape[1:])

    def scaled(m, j):
        for n, v in layout(pieces, m):
            cols = columns(n, v.shape[1])
            xn[j, :, cols] = (v * sc[j, :, 0:1] * gain_ref[:, cols]).astype(BF16)

    def picked(m, j):
        rows = dot(g_ref[m], xn[j]).astype(BF16)
        for i in range(experts):
            xs[i, pl.ds(aligned(m, CAP), CAP), :] = rows[i * CAP : (i + 1) * CAP]

    lap = xn.shape[0]

    def requests(i):
        for step in (squares, scaled, picked):
            for j in range(lap):
                step(i * lap + j, j)

    each(groups // lap, requests)
    for e in range(experts):
        for load in weights[e]:
            load.wait()
        if e == experts // 2:
            for load in [v for some in loads[1:] for v in some]:
                load.start()
        gate = dot(xs[e], gate_s[e])
        up = dot(xs[e], up_s[e])
        active = gate / (1.0 + jnp.exp(-gate)) * up
        active_ref[e] = (active * rw_ref[e, :, 0:1]).astype(BF16)
    for i, load in enumerate(loads[0]):
        load.wait()
        combine_rows(active_ref, down_s.at[i], c_ref, y_s, functools.partial(put, out_ref, i))
    for load in [v for some in loads[1:] for v in some]:
        load.wait()


def down_kernel(active_ref, c_ref, add_ref, down_ref, *refs, put):
    outs, y_s = refs[:-1], refs[-1]
    for i in range(down_ref.shape[0]):
        combine_rows(active_ref, down_ref.at[i], c_ref, y_s, functools.partial(put, outs, add_ref, i))


def put_plain(out_ref, i, m, value):
    out_ref[i, m] = value.astype(BF16)


def put_added(outs, add_ref, i, m, value):
    value = (value + add_ref[i, m].astype(F32)).astype(BF16)
    side, z = 2 * i + m // 4, m % 4
    if z == 0:
        outs[side][...] = value
    else:
        outs[4 + side][z - 1] = value


def total_kernel(own_ref, x_ref, y_ref, d_ref, mark_ref, *outs):
    for z in range(3):
        total = own_ref[z].astype(F32) + x_ref[z].astype(F32) + y_ref[z].astype(F32) + d_ref[z].astype(F32)
        outs[z][...] = total.astype(BF16)


def on_device(
    queries,
    draft_keys,
    draft_values,
    key_cache,
    value_cache,
    page_request,
    page_slot,
    cache_len,
    tree_mask,
    accepted,
    hidden_in,
    out_proj,
    norm_gain,
    gate_proj,
    up_proj,
    down_proj,
    expert_ids,
    route_weight,
):
    draft, width = queries.shape
    pages, page_len, _ = key_cache.shape
    model = hidden_in.shape[1]
    heads = width // HD
    seq, tensor = lax.axis_size("seq"), lax.axis_size("tensor")
    experts = gate_proj.shape[0]
    hidden = gate_proj.shape[2]
    accept = accepted.shape[1]
    slots = seq * CAP
    staged = seq == 8 and tensor == 4
    me, t = lax.axis_index("seq"), lax.axis_index("tensor")

    def hop(axis, mask):
        size = seq if axis == "seq" else tensor
        pairs = [(i, i ^ mask) for i in range(size)]
        return lambda v: lax.ppermute(v, axis, pairs)

    x1, y1, core = hop("seq", 1), hop("tensor", 2), hop("tensor", 1)
    zs = [hop("seq", 2 * k) for k in (1, 2, 3)]
    big = 16 if staged else 56

    def diagonal(v):
        flip = tensor + 2
        return lax.ppermute(v, ("seq", "tensor"), [(i, i ^ flip) for i in range(seq * tensor)])

    relative = page_request ^ me if staged else page_request
    pos = (relative & 1) * 4 + (relative >> 1) if staged else relative
    pos = pos.astype(I32)
    request_hit = page_request[:, None] == jnp.arange(cache_len.shape[0], dtype=I32)[None, :]
    live = jnp.sum(jnp.where(request_hit, cache_len[None, :], 0), axis=1) - page_slot * page_len
    me1, t1 = me.reshape(1).astype(I32), t.reshape(1).astype(I32)

    if staged:
        own = queries[None]
        line = [z(own) for z in zs]
        beside = x1(own)
        every_query = [own, *line, beside, *[x1(b) for b in line]]
    else:
        every_query = [lax.all_gather(queries[None], "seq", axis=0, tiled=True)]
    counts = tuple(a.shape[0] for a in every_query)

    near_out, near_lse, info, keys, values = call(
        near_kernel,
        "near",
        (
            queries,
            draft_keys,
            draft_values,
            tree_mask,
            key_cache,
            value_cache,
            accepted,
            expert_ids.T,
            route_weight.T,
        ),
        [hbm()] * 6 + [vmem()] * 3,
        [
            shape((draft, width), F32),
            shape((draft, width), F32),
            shape((draft, EXTRA), F32),
            shape(key_cache.shape, BF16),
            shape(value_cache.shape, BF16),
        ],
        [vmem()] * 5,
        [
            *[pltpu.VMEM((draft, width), BF16)] * 3,
            pltpu.VMEM((1, draft, draft), I32),
            pltpu.VMEM((heads, draft, draft), F32),
            pltpu.VMEM((heads, draft, draft), BF16),
            pltpu.SemaphoreType.DMA((6,)),
        ],
        busy=2,
    )

    n_out = seq if staged else 1
    state = pltpu.VMEM((seq, draft, width), F32)
    per_page = pltpu.VMEM((pages, draft, width), F32)
    partials = call(
        functools.partial(far_kernel, counts=counts, n_out=n_out),
        "far",
        (pos, live, keys, values, info, *every_query),
        [smem(), smem()] + [vmem()] * (3 + len(every_query)),
        [shape((seq // n_out, draft, width + EXTRA), BF16)] * n_out,
        [vmem()] * n_out,
        [pltpu.VMEM((seq, draft, width), BF16), *[per_page] * 4, *[state] * 3],
        limit=big,
        busy=5,
    )

    if staged:
        back = [partials[0]]
        for place in range(1, 8):
            back.append(hop("seq", (place & 3) * 2 + (place >> 2))(partials[place]))
    else:
        back = [lax.all_to_all(partials[0], "seq", split_axis=0, concat_axis=0, tiled=True)]

    n_parts = tensor if staged else 1
    part_shape = (
        [shape((draft, width), F32)] + [shape((draft, width), BF16)] * 3 if staged else [shape((draft, model), F32)]
    )
    back_counts = tuple(b.shape[0] for b in back)
    log_sum_exp, *parts = call(
        functools.partial(merge_kernel, counts=back_counts, n_out=n_parts),
        "merge",
        (t1, near_out, near_lse, hidden_in, out_proj, *back),
        [smem()] + [vmem()] * (4 + len(back)),
        [shape((draft, heads), F32)] + part_shape,
        [vmem()] * (1 + n_parts),
        limit=big,
        busy=4,
    )

    grouped, combine, slot_weight = call(
        functools.partial(slots_kernel, counts=back_counts, picks=expert_ids.shape[1], at_column=width),
        "slots",
        (me1, parts[0], *back),
        [smem(), vmem()] + [vmem()] * len(back),
        [
            shape((seq, experts * CAP, draft), BF16),
            shape((seq, draft, experts * CAP), BF16),
            shape((experts, slots, 128), F32),
        ],
        [vmem()] * 3,
        limit=big,
    )

    if staged:
        got = [hop("tensor", n)(parts[n]) for n in (1, 2, 3)]
        mixed, row = call(
            mix_kernel,
            "mix",
            (parts[0], *got, grouped),
            [vmem()] * 5,
            [shape((draft, width), F32), shape((1, draft, width), BF16)],
            [vmem()] * 2,
            busy=1,
        )
    else:
        summed = lax.psum(parts[0], "tensor") + hidden_in.astype(F32)
        mixed = lax.dynamic_slice_in_dim(summed, t * width, width, 1)
        row = mixed.astype(BF16)[None]

    if staged:
        line = [z(row) for z in zs]
        near_by = [row, x1(row), y1(row), diagonal(row)]
        line = call(
            stack_kernel, "stack", line, [vmem()] * 3, shape((3, draft, width), BF16), vmem(), limit=1, busy=0
        )
        far_off = [line, x1(line), y1(line), diagonal(line)]
        rows_in = near_by + far_off + [core(jnp.concatenate(near_by))] + [core(v) for v in far_off]

        def layout(refs, m):
            found = []
            for n in range(4):
                side, z = (n >> 1) * 2 + m // 4, m % 4
                if n & 1:
                    v = refs[8][side] if z == 0 else refs[9 + side][z - 1]
                else:
                    v = refs[side][0] if z == 0 else refs[4 + side][z - 1]
                found.append((n, v.astype(F32)))
            return found

        columns, steps, n_down = jnp.stack([t ^ 1, t ^ 3, t, t ^ 2]).astype(I32), (0, 2), 2
    else:
        rows_in = lax.all_gather(row, "seq", axis=0, tiled=True)
        rows_in = [lax.all_gather(rows_in, "tensor", axis=2, tiled=True)]

        def layout(refs, m):
            return [(None, refs[0][m].astype(F32))]

        columns, steps, n_down = jnp.arange(tensor, dtype=I32), (0,), tensor

    y_scratch = pltpu.VMEM((seq, experts * CAP, width), BF16)
    down_block = (n_down, experts, hidden, width)
    later = [shape(down_block, BF16)] * (len(steps) - 1)
    lap = math.gcd(seq, 8)
    active, sums, *later = call(
        functools.partial(expert_kernel, layout=layout, put=put_plain, steps=steps),
        "experts",
        (
            t1,
            columns,
            norm_gain.reshape(1, model),
            grouped,
            slot_weight,
            combine,
            gate_proj,
            up_proj,
            down_proj,
            *rows_in,
        ),
        [smem()] * 2 + [vmem()] * 4 + [hbm()] * 3 + [vmem()] * len(rows_in),
        [
            shape((experts, slots, hidden), BF16),
            shape((n_down, seq, draft, width), BF16),
            *later,
        ],
        [vmem()] * (2 + len(later)),
        [
            pltpu.VMEM((experts, slots, model), BF16),
            pltpu.VMEM((lap, draft, model), BF16),
            pltpu.VMEM((lap, draft, 128), F32),
            pltpu.VMEM(down_block, BF16),
            y_scratch,
            *[pltpu.VMEM((experts, model, hidden), BF16)] * 2,
            *[pltpu.SemaphoreType.DMA((experts,))] * 2,
            *[pltpu.SemaphoreType.DMA((n_down,))] * len(steps),
        ],
        limit=36 if staged else 60,
        busy=9,
    )

    if staged:
        sums = call(
            functools.partial(down_kernel, put=put_added),
            "down",
            (active, combine, core(sums), *later),
            [vmem()] * 4,
            [shape((draft, width), BF16)] * 4 + [shape((3, draft, width), BF16)] * 4,
            [vmem()] * 8,
            [y_scratch],
            busy=3,
        )
        first_sums = sums[0]
    else:
        first_sums = sums
    block = 4 if pages % 4 == 0 else 1
    page_spec = pl.BlockSpec((block, page_len, width), lambda p: (p, 0, 0))
    key_cache_out, value_cache_out, cache_mark = pl.pallas_call(
        functools.partial(cache_kernel, counts=back_counts, accept=accept),
        grid=(pages // block,),
        out_shape=[shape(key_cache.shape, BF16), shape(value_cache.shape, BF16), shape((8, 128), F32)],
        in_specs=[smem(), smem(), page_spec, page_spec, vmem()] + [vmem()] * len(back),
        out_specs=[page_spec, page_spec, pl.BlockSpec((8, 128), lambda p: (0, 0))],
        scratch_shapes=[pltpu.VMEM((seq, 2 * accept, width), BF16)],
        compiler_params=pltpu.CompilerParams(vmem_limit_bytes=big * MIB),
        cost_estimate=pl.CostEstimate(flops=0, bytes_accessed=12_000_000, transcendentals=0),
        name="cache",
    )(pos, live, in_hbm(key_cache), in_hbm(value_cache), first_sums, *back)

    if not staged:
        sums = lax.psum_scatter(sums, "tensor", scatter_dimension=0, tiled=True)[0]
        moe = lax.psum_scatter(sums, "seq", scatter_dimension=0, tiled=True)[0]
        mixed_out = (mixed + moe.astype(F32)).astype(BF16)
        return mixed_out, log_sum_exp, key_cache_out, value_cache_out

    line = call(
        total_kernel,
        "total",
        (sums[4], x1(sums[5]), y1(sums[6]), diagonal(sums[7]), cache_mark),
        [vmem()] * 5,
        [shape((draft, width), BF16)] * 3,
        [vmem()] * 3,
        busy=1,
    )
    moe = sums[0].astype(F32)
    for z, v in zip(zs, line):
        moe = moe + z(v).astype(F32)
    for move, v in zip((x1, y1, diagonal), sums[1:4]):
        moe = moe + move(v).astype(F32)
    mixed_out = (mixed + moe).astype(BF16)
    return mixed_out, log_sum_exp, key_cache_out, value_cache_out


def solution(mesh):
    return jax.shard_map(
        on_device,
        mesh=mesh,
        in_specs=(
            P("seq", "tensor"),
            P("seq", "tensor"),
            P("seq", "tensor"),
            P("seq", None, "tensor"),
            P("seq", None, "tensor"),
            P("seq"),
            P("seq"),
            P(),
            P("seq", None, None),
            P("seq", None),
            P("seq", None),
            P("tensor", None),
            P(),
            P("seq", None, "tensor"),
            P("seq", None, "tensor"),
            P("seq", "tensor", None),
            P("seq", None),
            P("seq", None),
        ),
        out_specs=(
            P("seq", "tensor"),
            P("seq", "tensor"),
            P("seq", None, "tensor"),
            P("seq", None, "tensor"),
        ),
        check_vma=False,
    )
```

```python
import functools
import math

import jax
import jax.numpy as jnp
from jax import lax
from jax.experimental import pallas as pl
from jax.experimental.pallas import tpu as pltpu
from jax.sharding import PartitionSpec as P

HD = 128
CAP = 16
MASKED = -1e30
F32 = jnp.float32
BF16 = jnp.bfloat16
I32 = jnp.int32
STAT = 128
INFO = 16
EXTRA = 256
MIB = 1024 * 1024


def vmem():
    return pl.BlockSpec(memory_space=pltpu.VMEM)


def hbm():
    return pl.BlockSpec(memory_space=pltpu.HBM)


def smem():
    return pl.BlockSpec(memory_space=pltpu.SMEM)


def shape(dims, dtype):
    return jax.ShapeDtypeStruct(dims, dtype)


def in_hbm(v):
    return pltpu.with_memory_space_constraint(v, pltpu.HBM)


def call(kernel, name, ins, in_specs, out_shape, out_specs, scratch=(), limit=16, busy=3):
    ins = [
        in_hbm(v) if spec.memory_space is pltpu.HBM else v
        for v, spec in zip(ins, in_specs)
    ]
    return pl.pallas_call(
        kernel,
        out_shape=out_shape,
        in_specs=in_specs,
        out_specs=out_specs,
        scratch_shapes=list(scratch),
        compiler_params=pltpu.CompilerParams(vmem_limit_bytes=limit * MIB),
        cost_estimate=pl.CostEstimate(flops=0, bytes_accessed=busy * 3_000_000, transcendentals=0),
        name=name,
    )(*ins)


def each(count, body):
    if count <= 16:
        for i in range(count):
            body(i)
    else:

        @pl.loop(0, count)
        def _(i):
            body(i)


def dot(a, b):
    return jnp.dot(a, b, preferred_element_type=F32)


def dot_t(a, b):
    return lax.dot_general(a, b, (((1,), (1,)), ((), ())), preferred_element_type=F32)


def dot_0(a, b):
    return lax.dot_general(a, b, (((0,), (0,)), ((), ())), preferred_element_type=F32)


def aligned(index, size):
    return index * size if isinstance(index, int) else pl.multiple_of(index * size, size)


def three_parts(value):
    high = value.astype(BF16).astype(F32)
    rest = value - high
    middle = rest.astype(BF16).astype(F32)
    return high, middle, rest - middle


def near_kernel(
    q_hbm, k_hbm, v_hbm, mask_hbm, key_hbm, value_hbm, acc_ref, ids_ref, rw_ref, *refs
):
    out_ref, lse_ref, info_ref, key_ref, value_ref, q_ref, k_ref, v_ref, mask_ref, s_s, w_s, sems = refs
    loads = [
        pltpu.make_async_copy(source, target, sems.at[i])
        for i, (source, target) in enumerate(
            (
                (q_hbm, q_ref),
                (k_hbm, k_ref),
                (v_hbm, v_ref),
                (mask_hbm, mask_ref),
                (key_hbm, key_ref),
                (value_hbm, value_ref),
            )
        )
    ]
    for load in loads:
        load.start()
    for load in loads[:4]:
        load.wait()
    draft, width = q_ref.shape
    scaling = 1.0 / math.sqrt(HD)
    seen = mask_ref[0] > 0
    heads = [slice(h * HD, (h + 1) * HD) for h in range(width // HD)]
    for h, cols in enumerate(heads):
        s_s[h] = jnp.where(seen, dot_t(q_ref[:, cols], k_ref[:, cols]) * scaling, MASKED)
    for h, cols in enumerate(heads):
        lse_ref[:, cols] = jnp.broadcast_to(jnp.max(s_s[h], axis=1, keepdims=True), (draft, HD))
    for h, cols in enumerate(heads):
        top = lse_ref[:, cols]
        weights = jnp.exp(s_s[h] - top[:, 0:draft])
        total = jnp.sum(weights, axis=1, keepdims=True)
        w_s[h] = (weights / total).astype(BF16)
        lse_ref[:, cols] = top + jnp.log(jnp.broadcast_to(total, (draft, HD)))
    for h, cols in enumerate(heads):
        out_ref[:, cols] = dot(w_s[h], v_ref[:, cols])
    accepted = acc_ref.shape[1]
    pick = (lax.broadcasted_iota(I32, (draft, accepted), 0) == acc_ref[...]).astype(F32).astype(BF16)
    rows = jnp.concatenate([dot_0(pick, k_ref[...]), dot_0(pick, v_ref[...])], axis=0)
    picks = ids_ref.shape[0]
    info = jnp.zeros((draft, STAT), F32)
    for g, part in enumerate((ids_ref[...].astype(F32), *three_parts(rw_ref[...]))):
        lane = lax.broadcasted_iota(I32, (picks, STAT), 1) - INFO - g * picks
        spread = jnp.where(lane == lax.broadcasted_iota(I32, (picks, STAT), 0), 1.0, 0.0)
        info = info + dot_0(part.astype(BF16), spread.astype(BF16))
    info_ref[:, 0:STAT] = info
    for g in range(width // 128):
        part = rows[:, g * 128 : (g + 1) * 128]
        info_ref[g * 2 * accepted : (g + 1) * 2 * accepted, STAT:] = part
    for load in loads[4:]:
        load.wait()


def far_kernel(pos_ref, live_ref, key_ref, value_ref, info_ref, *refs, counts, n_out):
    pieces, outs = refs[: len(counts)], refs[len(counts) : len(counts) + n_out]
    q_s, s_s, mp_s, lp_s, op_s, m_s, l_s, o_s = refs[len(counts) + n_out :]
    pages, page_len, width = key_ref.shape
    draft = q_s.shape[1]
    heads = width // HD
    scaling = 1.0 / math.sqrt(HD)
    at = 0
    for piece, count in zip(pieces, counts):
        q_s[at : at + count] = piece[...]
        at += count
    cell = lax.broadcasted_iota(I32, (draft, page_len), 1)
    pairs = [(p, slice(h * HD, (h + 1) * HD)) for p in range(pages) for h in range(heads)]
    for p, cols in pairs:
        scores = dot_t(q_s[pos_ref[p], :, cols], key_ref[p, :, cols]) * scaling
        s_s[p, :, cols] = jnp.where(cell < live_ref[p], scores, MASKED)
    for p, cols in pairs:
        mp_s[p, :, cols] = jnp.broadcast_to(jnp.max(s_s[p, :, cols], axis=1, keepdims=True), (draft, HD))
    for p, cols in pairs:
        weights = jnp.exp(s_s[p, :, cols] - mp_s[p, :, cols])
        lp_s[p, :, cols] = jnp.broadcast_to(jnp.sum(weights, axis=1, keepdims=True), (draft, HD))
        op_s[p, :, cols] = dot(weights.astype(BF16), value_ref[p, :, cols])

    def clear(i):
        m_s[i] = jnp.full((draft, width), MASKED, F32)
        l_s[i] = jnp.zeros((draft, width), F32)
        o_s[i] = jnp.zeros((draft, width), F32)

    each(at, clear)
    for p in range(pages):
        pos = pos_ref[p]
        m_s[pos] = jnp.maximum(m_s[pos], mp_s[p])
    for p in range(pages):
        pos = pos_ref[p]
        scale = jnp.exp(mp_s[p] - m_s[pos])
        l_s[pos] = l_s[pos] + lp_s[p] * scale
        o_s[pos] = o_s[pos] + op_s[p] * scale
    lane = lax.broadcasted_iota(I32, (draft, STAT), 1)

    def finish(i):
        target, row = (outs[i], 0) if n_out > 1 else (outs[0], i)
        stat = jnp.zeros((draft, STAT), F32)
        for h in range(heads):
            cols = slice(h * HD, (h + 1) * HD)
            total = l_s[i, :, cols]
            some = total > 0.0
            safe = jnp.where(some, total, 1.0)
            target[row, :, cols] = (o_s[i, :, cols] / safe).astype(BF16)
            lse = jnp.where(some, m_s[i, :, cols] + jnp.log(safe), MASKED)
            stat = jnp.where(lane % heads == h, lse, stat)
        high, middle, low = three_parts(stat)
        packed = jnp.where(lane < heads, high, jnp.where(lane < 2 * heads, middle, low))
        packed = jnp.where(lane < 3 * heads, packed, info_ref[:, 0:STAT])
        target[row, :, width : width + STAT] = packed.astype(BF16)
        target[row, :, width + STAT :] = info_ref[:, STAT:].astype(BF16)

    each(at, finish)


def merge_kernel(t_ref, near_ref, lse_ref, hidden_ref, w_ref, *refs, counts, n_out):
    pieces, refs = refs[: len(counts)], refs[len(counts) :]
    lse_out, outs = refs[0], refs[1:]
    draft, width = near_ref.shape
    heads = width // HD
    rows = [(piece, i) for piece, count in zip(pieces, counts) for i in range(count)]
    stats = []
    for piece, i in rows:
        packed = piece[i, :, width : width + STAT].astype(F32)
        stats.append(packed + pltpu.roll(packed, STAT - heads, 1) + pltpu.roll(packed, STAT - 2 * heads, 1))
    attended = []
    for h in range(heads):
        cols = slice(h * HD, (h + 1) * HD)
        sums = [s[:, h : h + 1] for s in stats]
        own = lse_ref[:, h * HD : h * HD + 1]
        top = functools.reduce(jnp.maximum, sums, own)
        weight = jnp.exp(own - top)
        total = weight
        summed = near_ref[:, cols] * weight
        for (piece, i), s in zip(rows, sums):
            weight = jnp.exp(s - top)
            total = total + weight
            summed = summed + piece[i, :, cols].astype(F32) * weight
        attended.append((summed / total).astype(BF16))
        lse_out[:, h : h + 1] = top + jnp.log(total)
    attended = jnp.concatenate(attended, axis=1)
    if n_out == 1:
        outs[0][...] = dot(attended, w_ref[...]).astype(outs[0].dtype)
        return
    for n in range(n_out):
        start = pl.multiple_of((t_ref[0] ^ n) * width, width)
        part = dot(attended, w_ref[:, pl.ds(start, width)])
        if n == 0:
            part = part + hidden_ref[:, pl.ds(start, width)].astype(F32)
        outs[n][...] = part.astype(outs[n].dtype)


def slots_kernel(me_ref, after_ref, *refs, counts, picks, at_column):
    pieces, (g_ref, c_ref, w_ref) = refs[: len(counts)], refs[len(counts) :]
    draft = g_ref.shape[2]
    experts = w_ref.shape[0]
    row, column = (lax.broadcasted_iota(I32, (draft, draft), axis) for axis in (0, 1))
    upper = jnp.where(row < column, 1.0, 0.0).astype(BF16)
    same = jnp.where(row == column, 1.0, 0.0).astype(BF16)
    number = lax.broadcasted_iota(I32, (CAP, draft), 0).astype(F32)
    first = me_ref[0] * experts

    def one(piece, i, m):
        info = jnp.transpose(piece[i, :, at_column : at_column + STAT].astype(F32))
        ids, *parts = (info[INFO + g * picks : INFO + (g + 1) * picks] for g in range(4))
        weight = parts[0] + parts[1] + parts[2]
        hits, weights = [], []
        for e in range(experts):
            hit = ids == (first + e).astype(F32)
            hits.append(jnp.max(jnp.where(hit, 1.0, 0.0), axis=0, keepdims=True))
            weights.append(jnp.sum(jnp.where(hit, weight, 0.0), axis=0, keepdims=True))
        table = jnp.concatenate(hits + [jnp.zeros((16 - experts, draft), F32)], axis=0)
        rank = dot(table.astype(BF16), upper)
        blocks = []
        for e in range(experts):
            block = jnp.where((number == rank[e : e + 1]) & (hits[e] > 0.0), 1.0, 0.0)
            blocks.append(block)
            row_weight = jnp.sum(block * weights[e], axis=1, keepdims=True)
            w_ref[e, pl.ds(aligned(m, CAP), CAP), :] = jnp.broadcast_to(row_weight, (CAP, 128))
        stacked = jnp.concatenate(blocks, axis=0).astype(BF16)
        g_ref[m] = stacked
        c_ref[m] = dot_t(same, stacked).astype(BF16)

    at = 0
    for piece, count in zip(pieces, counts):
        each(count, lambda i, piece=piece, at=at: one(piece, i, at + i))
        at += count


def mix_kernel(own_ref, a_ref, b_ref, c_ref, after_ref, mixed_ref, row_ref):
    mixed = own_ref[...] + a_ref[...].astype(F32) + b_ref[...].astype(F32) + c_ref[...].astype(F32)
    mixed_ref[...] = mixed
    row_ref[0] = mixed.astype(BF16)


def cache_kernel(pos_ref, live_ref, key_ref, value_ref, after_ref, *refs, counts, accept):
    pieces, (key_out, value_out, mark_ref, table) = refs[: len(counts)], refs[len(counts) :]
    block, page_len, width = key_ref.shape
    step = pl.program_id(0)

    @pl.when(step == 0)
    def _():
        at = 0
        for piece, count in zip(pieces, counts):
            for g in range(width // 128):
                rows = slice(g * 2 * accept, (g + 1) * 2 * accept)
                table[at : at + count, :, g * 128 : (g + 1) * 128] = piece[:, rows, width + STAT :]
            at += count
        mark_ref[...] = jnp.zeros_like(mark_ref)

    key_out[...] = key_ref[...]
    value_out[...] = value_ref[...]
    for i in range(block):
        p = step * block + i
        live = live_ref[p]

        @pl.when((live > -accept) & (live < page_len))
        def _():
            rows = table[pos_ref[p]]
            offset = lax.broadcasted_iota(I32, (page_len, 2 * accept), 0) - live
            column = lax.broadcasted_iota(I32, (page_len, 2 * accept), 1)
            cell = lax.broadcasted_iota(I32, (page_len, width), 0) - live
            touched = (cell >= 0) & (cell < accept)
            for source, out, shift in ((key_ref, key_out, 0), (value_ref, value_out, accept)):
                hit = (offset == column - shift) & (offset >= 0) & (offset < accept)
                place = jnp.where(hit, 1.0, 0.0).astype(BF16)
                out[i] = jnp.where(touched, dot(place, rows), source[i].astype(F32)).astype(BF16)


def combine_rows(active_ref, down_ref, c_ref, y_s, put):
    experts = active_ref.shape[0]
    groups = c_ref.shape[0]
    for e in range(experts):
        y = dot(active_ref[e], down_ref[e]).astype(BF16)
        for m in range(groups):
            y_s[m, e * CAP : (e + 1) * CAP, :] = y[m * CAP : (m + 1) * CAP]
    each(groups, lambda m: put(m, dot(c_ref[m], y_s[m])))


def down_loads(cols_ref, first, down_hbm, down_s, sems):
    width = down_s.shape[3]
    loads = []
    for i in range(down_s.shape[0]):
        cols = pl.ds(pl.multiple_of(cols_ref[first + i] * width, width), width)
        loads.append(pltpu.make_async_copy(down_hbm.at[:, :, cols], down_s.at[i], sems.at[i]))
    return loads


def stack_kernel(*refs):
    for i, block in enumerate(refs[:-1]):
        refs[-1][i] = block[0]


def expert_kernel(
    t_ref, cols_ref, gain_ref, g_ref, rw_ref, c_ref, gate_hbm, up_hbm, down_hbm, *refs, layout, put, steps
):
    later = len(steps) - 1
    pieces, refs = refs[: -10 - 2 * len(steps)], refs[-10 - 2 * len(steps) :]
    active_ref, out_ref, refs = refs[0], refs[1], refs[2:]
    later, (xs, xn, sc, down_s, y_s, gate_s, up_s, gate_sem, up_sem, *sems) = refs[:later], refs[later:]
    experts, slots, model = xs.shape
    groups = g_ref.shape[0]
    weights = [
        (
            pltpu.make_async_copy(gate_hbm.at[e], gate_s.at[e], gate_sem.at[e]),
            pltpu.make_async_copy(up_hbm.at[e], up_s.at[e], up_sem.at[e]),
        )
        for e in range(experts)
    ]
    buffers = [down_s, *later]
    loads = [down_loads(cols_ref, first, down_hbm, to, sem) for first, to, sem in zip(steps, buffers, sems)]
    for some in weights:
        for load in some:
            load.start()
    for load in loads[0]:
        load.start()

    def columns(n, width):
        return slice(0, width) if n is None else pl.ds(pl.multiple_of((t_ref[0] ^ n) * width, width), width)

    def squares(m, j):
        total = sum(jnp.sum(v * v, axis=1, keepdims=True) for _, v in layout(pieces, m))
        sc[j] = jnp.broadcast_to(lax.rsqrt(total / model + 1e-6), sc.shape[1:])

    def scaled(m, j):
        for n, v in layout(pieces, m):
            cols = columns(n, v.shape[1])
            xn[j, :, cols] = (v * sc[j, :, 0:1] * gain_ref[:, cols]).astype(BF16)

    def picked(m, j):
        rows = dot(g_ref[m], xn[j]).astype(BF16)
        for i in range(experts):
            xs[i, pl.ds(aligned(m, CAP), CAP), :] = rows[i * CAP : (i + 1) * CAP]

    lap = xn.shape[0]

    def requests(i):
        for step in (squares, scaled, picked):
            for j in range(lap):
                step(i * lap + j, j)

    each(groups // lap, requests)
    for e in range(experts):
        for load in weights[e]:
            load.wait()
        if e == experts // 2:
            for load in [v for some in loads[1:] for v in some]:
                load.start()
        gate = dot(xs[e], gate_s[e])
        up = dot(xs[e], up_s[e])
        active = gate / (1.0 + jnp.exp(-gate)) * up
        active_ref[e] = (active * rw_ref[e, :, 0:1]).astype(BF16)
    for i, load in enumerate(loads[0]):
        load.wait()
        combine_rows(active_ref, down_s.at[i], c_ref, y_s, functools.partial(put, out_ref, i))
    for load in [v for some in loads[1:] for v in some]:
        load.wait()


def down_kernel(active_ref, c_ref, down_ref, out_ref, y_s, *, put):
    for i in range(down_ref.shape[0]):
        combine_rows(active_ref, down_ref.at[i], c_ref, y_s, functools.partial(put, out_ref, i))


def put_rows(out_ref, i, m, value):
    out_ref[i, m] = value.astype(out_ref.dtype)


def split_kernel(own_ref, add_ref, *outs):
    for side in range(4):
        for z in range(4):
            at = (side // 2, side % 2 * 4 + z)
            value = (own_ref[at] + add_ref[at].astype(F32)).astype(BF16)
            if z == 0:
                outs[side][...] = value
            else:
                outs[4 + side][z - 1] = value


def total_kernel(own_ref, x_ref, y_ref, d_ref, mark_ref, *outs):
    for z in range(3):
        total = own_ref[z].astype(F32) + x_ref[z].astype(F32) + y_ref[z].astype(F32) + d_ref[z].astype(F32)
        outs[z][...] = total.astype(BF16)


def on_device(
    queries,
    draft_keys,
    draft_values,
    key_cache,
    value_cache,
    page_request,
    page_slot,
    cache_len,
    tree_mask,
    accepted,
    hidden_in,
    out_proj,
    norm_gain,
    gate_proj,
    up_proj,
    down_proj,
    expert_ids,
    route_weight,
):
    draft, width = queries.shape
    pages, page_len, _ = key_cache.shape
    model = hidden_in.shape[1]
    heads = width // HD
    seq, tensor = lax.axis_size("seq"), lax.axis_size("tensor")
    experts = gate_proj.shape[0]
    hidden = gate_proj.shape[2]
    accept = accepted.shape[1]
    slots = seq * CAP
    staged = seq == 8 and tensor == 4
    me, t = lax.axis_index("seq"), lax.axis_index("tensor")

    def hop(axis, mask):
        size = seq if axis == "seq" else tensor
        pairs = [(i, i ^ mask) for i in range(size)]
        return lambda v: lax.ppermute(v, axis, pairs)

    x1, y1, core = hop("seq", 1), hop("tensor", 2), hop("tensor", 1)
    zs = [hop("seq", 2 * k) for k in (1, 2, 3)]
    big = 16 if staged else 56

    def diagonal(v):
        flip = tensor + 2
        return lax.ppermute(v, ("seq", "tensor"), [(i, i ^ flip) for i in range(seq * tensor)])

    relative = page_request ^ me if staged else page_request
    pos = (relative & 1) * 4 + (relative >> 1) if staged else relative
    pos = pos.astype(I32)
    request_hit = page_request[:, None] == jnp.arange(cache_len.shape[0], dtype=I32)[None, :]
    live = jnp.sum(jnp.where(request_hit, cache_len[None, :], 0), axis=1) - page_slot * page_len
    me1, t1 = me.reshape(1).astype(I32), t.reshape(1).astype(I32)

    if staged:
        own = queries[None]
        line = [z(own) for z in zs]
        beside = x1(own)
        every_query = [own, *line, beside, *[x1(b) for b in line]]
    else:
        every_query = [lax.all_gather(queries[None], "seq", axis=0, tiled=True)]
    counts = tuple(a.shape[0] for a in every_query)

    near_out, near_lse, info, keys, values = call(
        near_kernel,
        "near",
        (
            queries,
            draft_keys,
            draft_values,
            tree_mask,
            key_cache,
            value_cache,
            accepted,
            expert_ids.T,
            route_weight.T,
        ),
        [hbm()] * 6 + [vmem()] * 3,
        [
            shape((draft, width), F32),
            shape((draft, width), F32),
            shape((draft, EXTRA), F32),
            shape(key_cache.shape, BF16),
            shape(value_cache.shape, BF16),
        ],
        [vmem()] * 5,
        [
            *[pltpu.VMEM((draft, width), BF16)] * 3,
            pltpu.VMEM((1, draft, draft), I32),
            pltpu.VMEM((heads, draft, draft), F32),
            pltpu.VMEM((heads, draft, draft), BF16),
            pltpu.SemaphoreType.DMA((6,)),
        ],
        busy=2,
    )

    n_out = seq if staged else 1
    state = pltpu.VMEM((seq, draft, width), F32)
    per_page = pltpu.VMEM((pages, draft, width), F32)
    partials = call(
        functools.partial(far_kernel, counts=counts, n_out=n_out),
        "far",
        (pos, live, keys, values, info, *every_query),
        [smem(), smem()] + [vmem()] * (3 + len(every_query)),
        [shape((seq // n_out, draft, width + EXTRA), BF16)] * n_out,
        [vmem()] * n_out,
        [pltpu.VMEM((seq, draft, width), BF16), *[per_page] * 4, *[state] * 3],
        limit=big,
        busy=5,
    )

    if staged:
        back = [partials[0]]
        for place in range(1, 8):
            back.append(hop("seq", (place & 3) * 2 + (place >> 2))(partials[place]))
    else:
        back = [lax.all_to_all(partials[0], "seq", split_axis=0, concat_axis=0, tiled=True)]

    n_parts = tensor if staged else 1
    part_shape = (
        [shape((draft, width), F32)] + [shape((draft, width), BF16)] * 3 if staged else [shape((draft, model), F32)]
    )
    back_counts = tuple(b.shape[0] for b in back)
    log_sum_exp, *parts = call(
        functools.partial(merge_kernel, counts=back_counts, n_out=n_parts),
        "merge",
        (t1, near_out, near_lse, hidden_in, out_proj, *back),
        [smem()] + [vmem()] * (4 + len(back)),
        [shape((draft, heads), F32)] + part_shape,
        [vmem()] * (1 + n_parts),
        limit=big,
        busy=4,
    )

    grouped, combine, slot_weight = call(
        functools.partial(slots_kernel, counts=back_counts, picks=expert_ids.shape[1], at_column=width),
        "slots",
        (me1, parts[0], *back),
        [smem(), vmem()] + [vmem()] * len(back),
        [
            shape((seq, experts * CAP, draft), BF16),
            shape((seq, draft, experts * CAP), BF16),
            shape((experts, slots, 128), F32),
        ],
        [vmem()] * 3,
        limit=big,
    )

    if staged:
        got = [hop("tensor", n)(parts[n]) for n in (1, 2, 3)]
        mixed, row = call(
            mix_kernel,
            "mix",
            (parts[0], *got, grouped),
            [vmem()] * 5,
            [shape((draft, width), F32), shape((1, draft, width), BF16)],
            [vmem()] * 2,
            busy=1,
        )
    else:
        summed = lax.psum(parts[0], "tensor") + hidden_in.astype(F32)
        mixed = lax.dynamic_slice_in_dim(summed, t * width, width, 1)
        row = mixed.astype(BF16)[None]

    if staged:
        line = [z(row) for z in zs]
        near_by = [row, x1(row), y1(row), diagonal(row)]
        line = call(
            stack_kernel, "stack", line, [vmem()] * 3, shape((3, draft, width), BF16), vmem(), limit=1, busy=0
        )
        far_off = [line, x1(line), y1(line), diagonal(line)]
        rows_in = near_by + far_off + [core(jnp.concatenate(near_by))] + [core(v) for v in far_off]

        def layout(refs, m):
            found = []
            for n in range(4):
                side, z = (n >> 1) * 2 + m // 4, m % 4
                if n & 1:
                    v = refs[8][side] if z == 0 else refs[9 + side][z - 1]
                else:
                    v = refs[side][0] if z == 0 else refs[4 + side][z - 1]
                found.append((n, v.astype(F32)))
            return found

        columns, steps, n_down = jnp.stack([t ^ 1, t ^ 3, t, t ^ 2]).astype(I32), (0, 2), 2
    else:
        rows_in = lax.all_gather(row, "seq", axis=0, tiled=True)
        rows_in = [lax.all_gather(rows_in, "tensor", axis=2, tiled=True)]

        def layout(refs, m):
            return [(None, refs[0][m].astype(F32))]

        columns, steps, n_down = jnp.arange(tensor, dtype=I32), (0,), tensor

    y_scratch = pltpu.VMEM((seq, experts * CAP, width), BF16)
    down_block = (n_down, experts, hidden, width)
    later = [shape(down_block, BF16)] * (len(steps) - 1)
    lap = math.gcd(seq, 8)
    active, sums, *later = call(
        functools.partial(expert_kernel, layout=layout, put=put_rows, steps=steps),
        "experts",
        (
            t1,
            columns,
            norm_gain.reshape(1, model),
            grouped,
            slot_weight,
            combine,
            gate_proj,
            up_proj,
            down_proj,
            *rows_in,
        ),
        [smem()] * 2 + [vmem()] * 4 + [hbm()] * 3 + [vmem()] * len(rows_in),
        [
            shape((experts, slots, hidden), BF16),
            shape((n_down, seq, draft, width), BF16),
            *later,
        ],
        [vmem()] * (2 + len(later)),
        [
            pltpu.VMEM((experts, slots, model), BF16),
            pltpu.VMEM((lap, draft, model), BF16),
            pltpu.VMEM((lap, draft, 128), F32),
            pltpu.VMEM(down_block, BF16),
            y_scratch,
            *[pltpu.VMEM((experts, model, hidden), BF16)] * 2,
            *[pltpu.SemaphoreType.DMA((experts,))] * 2,
            *[pltpu.SemaphoreType.DMA((n_down,))] * len(steps),
        ],
        limit=36 if staged else 60,
        busy=9,
    )

    if staged:
        other = core(sums)
        own = call(
            functools.partial(down_kernel, put=put_rows),
            "down",
            (active, combine, *later),
            [vmem()] * 3,
            shape((2, seq, draft, width), F32),
            vmem(),
            [y_scratch],
            busy=2,
        )
        sums = call(
            split_kernel,
            "split",
            (own, other),
            [vmem()] * 2,
            [shape((draft, width), BF16)] * 4 + [shape((3, draft, width), BF16)] * 4,
            [vmem()] * 8,
            limit=4,
            busy=1,
        )
        first_sums = sums[0]
    else:
        first_sums = sums
    block = 4 if pages % 4 == 0 else 1
    page_spec = pl.BlockSpec((block, page_len, width), lambda p: (p, 0, 0))
    key_cache_out, value_cache_out, cache_mark = pl.pallas_call(
        functools.partial(cache_kernel, counts=back_counts, accept=accept),
        grid=(pages // block,),
        out_shape=[shape(key_cache.shape, BF16), shape(value_cache.shape, BF16), shape((8, 128), F32)],
        in_specs=[smem(), smem(), page_spec, page_spec, vmem()] + [vmem()] * len(back),
        out_specs=[page_spec, page_spec, pl.BlockSpec((8, 128), lambda p: (0, 0))],
        scratch_shapes=[pltpu.VMEM((seq, 2 * accept, width), BF16)],
        compiler_params=pltpu.CompilerParams(vmem_limit_bytes=big * MIB),
        cost_estimate=pl.CostEstimate(flops=0, bytes_accessed=12_000_000, transcendentals=0),
        name="cache",
    )(pos, live, in_hbm(key_cache), in_hbm(value_cache), first_sums, *back)

    if not staged:
        sums = lax.psum_scatter(sums, "tensor", scatter_dimension=0, tiled=True)[0]
        moe = lax.psum_scatter(sums, "seq", scatter_dimension=0, tiled=True)[0]
        mixed_out = (mixed + moe.astype(F32)).astype(BF16)
        return mixed_out, log_sum_exp, key_cache_out, value_cache_out

    line = call(
        total_kernel,
        "total",
        (sums[4], x1(sums[5]), y1(sums[6]), diagonal(sums[7]), cache_mark),
        [vmem()] * 5,
        [shape((draft, width), BF16)] * 3,
        [vmem()] * 3,
        busy=1,
    )
    moe = sums[0].astype(F32)
    for z, v in zip(zs, line):
        moe = moe + z(v).astype(F32)
    for move, v in zip((x1, y1, diagonal), sums[1:4]):
        moe = moe + move(v).astype(F32)
    mixed_out = (mixed + moe).astype(BF16)
    return mixed_out, log_sum_exp, key_cache_out, value_cache_out


def solution(mesh):
    return jax.shard_map(
        on_device,
        mesh=mesh,
        in_specs=(
            P("seq", "tensor"),
            P("seq", "tensor"),
            P("seq", "tensor"),
            P("seq", None, "tensor"),
            P("seq", None, "tensor"),
            P("seq"),
            P("seq"),
            P(),
            P("seq", None, None),
            P("seq", None),
            P("seq", None),
            P("tensor", None),
            P(),
            P("seq", None, "tensor"),
            P("seq", None, "tensor"),
            P("seq", "tensor", None),
            P("seq", None),
            P("seq", None),
        ),
        out_specs=(
            P("seq", "tensor"),
            P("seq", "tensor"),
            P("seq", None, "tensor"),
            P("seq", None, "tensor"),
        ),
        check_vma=False,
    )
```
